128 devices in a mesh: lib: 8 (over y, x_hi), row: 4 (over z), col: 4 (over x_lo, core).
Axes of the slice: x: 4 (x_hi: 2, x_lo: 2; x = x_hi * 2 + x_lo), y: 4, z: 4, core: 2. Of those that a mesh axis runs over, the one named last changes fastest.
Arguments:
- abundance: float32 [1024, 128, 1024], P('lib', 'row', 'col'), may hold values from 0 to 1
- duals: float32 [2, 1024, 128, 1024], P(None, 'lib', 'row', 'col'), may hold values from -1 to 1
- reflectance: bfloat16 [224, 128, 1024], P(None, 'row', 'col'), may hold values from -6 to 6
- library: bfloat16 [224, 1024], P(None, 'lib'), may hold values from -0.375 to 0.375
Outputs:
- abund_next: float32 [1024, 128, 1024], P('lib', 'row', 'col')
- duals_next: float32 [2, 1024, 128, 1024], P(None, 'lib', 'row', 'col')
The draws below stay inside these ranges and needn't reach their ends.
All inputs are finite; a program needn't handle non-finite values.
Results may differ from the reference program's by a relative error of at most 0.0018.
Values may be sent and summed in bfloat16 or wider, within the bound.
No kernel may reach another device: no remote copies, remote signals or barrier semaphores. Data moves between devices by JAX's collectives and lax.ppermute only.
A program may use at most 192 MiB of HBM per device.

```python
import jax
import jax.numpy as jnp
from jax import lax

B = 224
M = 1024
PASSES = 3
NH = 128
NW = 1024


def steps_of(rng, extent, cuts, least, largest):
    factor_of = 1.0
    for axis_at, parts in cuts:
        draws = jax.random.uniform(jax.random.fold_in(jax.random.fold_in(rng, 6), axis_at), (parts,), jnp.float32, least / len(cuts), largest / len(cuts))
        factor_of = factor_of * jnp.repeat(jnp.exp(draws), extent[axis_at] // parts).reshape((-1,) + (1,) * (len(extent) - 1 - axis_at))
    return factor_of


def centred(rng, dims, spread, most, pieces=(), held_as=jnp.bfloat16):
    gain = steps_of(rng, dims, pieces, -0.22, 0.18) if pieces else 1.0
    result = jax.random.normal(rng, dims, jnp.float32) * spread * gain
    return jnp.minimum(jnp.maximum(result, -most), most).astype(held_as)


def setup_inputs(seed: int = 0) -> dict:
    keys = jax.random.split(jax.random.key(seed), 5)
    return {
        "abundance": jnp.clip(1.0 * jax.random.uniform(keys[0], (M, NH, NW), jnp.float32) ** steps_of(keys[0], (M, NH, NW), ((0, 8), (1, 4), (2, 4)), -0.2, 0.2), 0.0, 1.0),
        "duals": jnp.clip(jax.random.uniform(keys[1], (2, M, NH, NW), jnp.float32, -1.0, 1.0) * steps_of(keys[1], (2, M, NH, NW), ((1, 8), (2, 4), (3, 4)), -0.4, 0.0), -1.0, 1.0),
        "reflectance": centred(keys[2], (B, NH, NW), 1.0, 6.0, ((1, 4), (2, 4))),
        "library": centred(keys[3], (B, M), B ** -0.5, 0.375, ((1, 8),)),
    }


def divergence(dual):
    first = dual[0]
    second = dual[1]
    down = first - jnp.pad(first, ((0, 0), (1, 0), (0, 0)))[:, :-1, :]
    right = second - jnp.pad(second, ((0, 0), (0, 0), (1, 0)))[:, :, :-1]
    return down + right


def gradient(field):
    down = jnp.pad(field[:, 1:, :] - field[:, :-1, :], ((0, 0), (0, 1), (0, 0)))
    right = jnp.pad(field[:, :, 1:] - field[:, :, :-1], ((0, 0), (0, 0), (0, 1)))
    return jnp.stack([down, right])


def reference(abundance, duals, reflectance, library):
    flat = abundance.astype(jnp.bfloat16).reshape(M, NH * NW)
    resid = jnp.dot(library, flat, preferred_element_type=jnp.float32) - reflectance.reshape(B, NH * NW).astype(jnp.float32)
    descent = jnp.dot(library.T, resid.astype(jnp.bfloat16), preferred_element_type=jnp.float32)
    descent = descent.reshape(M, NH, NW).astype(abundance.dtype)
    keep_rows = (jnp.arange(NH) < NH - 1).astype(abundance.dtype)[:, None]
    keep_cols = (jnp.arange(NW) < NW - 1).astype(abundance.dtype)[None, :]
    group = min(M, 128)
    blocks = M // group

    def solve(items):
        current, direction, dual = items
        start = current - 0.1 * direction
        dual = jnp.stack([dual[0] * keep_rows, dual[1] * keep_cols])
        for step in range(PASSES):
            field = start - 0.25 * divergence(dual)
            dual = jnp.clip(dual + 0.5 * gradient(field), -1.0, 1.0)
        final = start - 0.25 * divergence(dual)
        return jnp.maximum(final - 0.02, 0.0), dual

    stacked = jnp.swapaxes(duals.reshape(2, blocks, group, NH, NW), 0, 1)
    abund_next, dual_next = lax.map(solve, (abundance.reshape(blocks, group, NH, NW), descent.reshape(blocks, group, NH, NW), stacked))
    abund_next = abund_next.reshape(M, NH, NW)
    dual_next = jnp.swapaxes(dual_next, 0, 1).reshape(2, M, NH, NW)
    return abund_next, dual_next
```

```python
import functools

import jax
import jax.numpy as jnp
from jax import lax
from jax.experimental import pallas as pl
from jax.experimental.pallas import tpu as pltpu
from jax.sharding import Mesh
from jax.sharding import PartitionSpec as P

PASSES = 3
LIB = ("lib_0", "lib_1")
BF16 = jnp.bfloat16
F32 = jnp.float32
LIMIT = 56 * 1024 * 1024
WHOLE = pl.BlockSpec(memory_space=pltpu.VMEM)
SCALARS = pl.BlockSpec(memory_space=pltpu.SMEM)
HOPS = ((2, 0), (2, 1), (1, 0), (3, 0), (1, 1), (3, 1), (0, 1))


def to_lib(array, hop):
    dy, dx = hop
    pairs = [(y * 2 + x, (y + dy) % 4 * 2 + (x ^ dx)) for y in range(4) for x in range(2)]
    return lax.ppermute(array, LIB, pairs)


def shifted(array, axis, by):
    length = lax.axis_size(axis)
    pairs = [(i, i + by) for i in range(length) if 0 <= i + by < length]
    return lax.ppermute(array, axis, pairs)


def shifted_both(array, down, right):
    rows, cols = lax.axis_size("row"), lax.axis_size("col")
    pairs = [
        (r * cols + c, (r + down) * cols + c + right)
        for r in range(rows)
        for c in range(cols)
        if 0 <= r + down < rows and 0 <= c + right < cols
    ]
    return lax.ppermute(array, ("row", "col"), pairs)


def resid_kernel(place, blocks_and_more):
    *blocks, library, observed, out = blocks_and_more
    for r in range(out.shape[0]):
        total = -observed[r].astype(F32)
        for k, block in enumerate(blocks):
            total += jnp.dot(library[place[k]], block[r], preferred_element_type=F32)
        out[r] = total.astype(BF16)


def residual(place, blocks, library, observed):
    return pl.pallas_call(
        lambda place, *refs: resid_kernel(place, refs),
        out_shape=jax.ShapeDtypeStruct(observed.shape, BF16),
        in_specs=[SCALARS] + [WHOLE] * (len(blocks) + 2),
        out_specs=WHOLE,
        compiler_params=pltpu.CompilerParams(vmem_limit_bytes=LIMIT),
        name="residual",
    )(place, *blocks, library, observed)


def gathered(mine):
    half = mine.shape[0] // 2
    a, b = mine[:half], mine[half:]
    up, down, across = (1, 0), (3, 0), (0, 1)
    bu, bd = to_lib(b, up), to_lib(b, down)
    ax = to_lib(a, across)
    au, ad = to_lib(a, up), to_lib(a, down)
    axu, axd = to_lib(ax, up), to_lib(ax, down)
    b2u, b2d = to_lib(bu[: half // 2], up), to_lib(bd[half // 2 :], down)
    a2, ax2 = to_lib(au, up), to_lib(axd, down)
    pieces = [
        (a, (0, 0), 0),
        (ax, (0, 1), 0),
        (au, (3, 0), 0),
        (ad, (1, 0), 0),
        (axu, (3, 1), 0),
        (axd, (1, 1), 0),
        (a2, (2, 0), 0),
        (ax2, (2, 1), 0),
    ]
    second = [
        (b, (0, 0), half),
        (bu, (3, 0), half),
        (bd, (1, 0), half),
        (b2u, (2, 0), half),
        (b2d, (2, 0), half + half // 2),
    ]
    pieces += second
    pieces += [(to_lib(v, across), (dy, 1), first) for v, (dy, _), first in second]
    return pieces


def descent_kernel(firsts, refs):
    *pieces, library_t, out = refs
    for k, piece in enumerate(pieces):
        for r in range(piece.shape[0]):
            d = jnp.dot(library_t[...], piece[r], preferred_element_type=F32)
            out[firsts[k] + r, 0] = d[:, :128]
            out[firsts[k] + r, 1] = d[:, 128:]


def descent(firsts, pieces, library_t, rows):
    maps = library_t.shape[0]
    return pl.pallas_call(
        lambda firsts, *refs: descent_kernel(firsts, refs),
        out_shape=jax.ShapeDtypeStruct((rows, 2, maps, 128), F32),
        in_specs=[SCALARS] + [WHOLE] * (len(pieces) + 1),
        out_specs=WHOLE,
        compiler_params=pltpu.CompilerParams(vmem_limit_bytes=LIMIT),
        cost_estimate=pl.CostEstimate(flops=2 * 224 * 128 * 8192, bytes_accessed=8_000_000, transcendentals=0),
        name="descent",
    )(firsts, *pieces, library_t)


def edges_kernel(d_ref, first_ref, last_ref, strip_ref):
    rows = d_ref.shape[0]
    first_ref[...] = d_ref[:4].astype(BF16)
    last_ref[...] = d_ref[rows - 4 :].astype(BF16)
    sub = lax.broadcasted_iota(jnp.int32, (8, 128), 0)

    def one(r, _):
        left = d_ref[r, 0].T[:8]
        right = d_ref[r, 1].T[120:]
        strip_ref[r] = pltpu.roll(jnp.where(sub < 4, left, right), 4, 0)
        return 0

    lax.fori_loop(0, rows, one, 0)


def edges(d):
    rows, _, maps, _ = d.shape
    band = jax.ShapeDtypeStruct((4, 2, maps, 128), BF16)
    return pl.pallas_call(
        edges_kernel,
        out_shape=(band, band, jax.ShapeDtypeStruct((rows, 8, maps), F32)),
        in_specs=[WHOLE],
        out_specs=(WHOLE,) * 3,
        compiler_params=pltpu.CompilerParams(vmem_limit_bytes=LIMIT),
        name="edges",
    )(d)


def below_then_above(array, dim, reach=4):
    size = array.shape[dim]
    below = shifted(lax.slice_in_dim(array, 0, reach, axis=dim), "row", -1)
    above = shifted(lax.slice_in_dim(array, size - reach, size, axis=dim), "row", 1)
    return lax.concatenate([below, above], dim)


def strips_two_steps(own):
    dim = own.ndim - 3
    tall = lax.concatenate([own, below_then_above(own, dim)], dim)
    return tall, shifted(tall, "col", 1), shifted(tall, "col", -1)


def strips_one_step(own):
    dim = own.ndim - 3
    rows = own.shape[dim]
    first = lax.slice_in_dim(own, 0, 4, axis=dim)
    last = lax.slice_in_dim(own, rows - 4, rows, axis=dim)

    def tall(right):
        middle = shifted(own, "col", right) if right else own
        return lax.concatenate(
            [middle, shifted_both(first, -1, right), shifted_both(last, 1, right)], dim
        )

    return tall(0), tall(1), tall(-1)


def tv_kernel(
    origin,
    ab_ref,
    q_ref,
    rim_ref,
    d_ref,
    drim_ref,
    own_ref,
    left_ref,
    right_ref,
    down_ref,
    dleft_ref,
    dright_ref,
    abn_ref,
    qn_ref,
    lefts,
    rights,
    turn,
):
    block, rows, _ = ab_ref.shape
    tall = rows + 8
    maps = own_ref.shape[-1]
    first_row, first_col, total_rows, total_cols = (origin[i] for i in range(4))

    def row_bound(shape, axis):
        r = lax.broadcasted_iota(jnp.int32, shape, axis)
        g = first_row + jnp.where(r < rows + 4, r, r - tall)
        return jnp.where((g >= 0) & (g < total_rows - 1), 1.0, 0.0).astype(F32)

    @pl.when(pl.program_id(0) == 0)
    def _():
        b0 = row_bound((tall, 8, maps), 0)
        sub = lax.broadcasted_iota(jnp.int32, (tall, 8, maps), 1)

        def strip(nearer, further, offset, is_left):
            def pick(i):
                return jnp.where(sub < 4, nearer[i], further[i])

            g = first_col + offset + sub
            b1 = jnp.where((g >= 0) & (g < total_cols - 1), 1.0, 0.0).astype(F32)
            s = pick(0) - 0.1 * pick(3)
            u, v = jnp.clip(pick(1), -b0, b0), jnp.clip(pick(2), -b1, b1)
            for p in range(PASSES):
                if is_left:
                    turn[...] = v.reshape(tall * 8, maps)
                    lefts[p] = turn[pl.ds(3, tall, 8), :]
                uu = jnp.concatenate([u[tall - 1 :], u[: tall - 1]], axis=0)
                z = s - 0.25 * (u - uu + (v - pltpu.roll(v, 1, 1)))
                if not is_left:
                    turn[...] = z.reshape(tall * 8, maps)
                    rights[p] = turn[pl.ds(4, tall, 8), :]
                zd = jnp.concatenate([z[1:], z[:1]], axis=0)
                zr = pltpu.roll(z, 7, 1)
                u = jnp.clip(u + 0.5 * (zd - z), -b0, b0)
                v = jnp.clip(v + 0.5 * (zr - z), -b1, b1)
            if is_left:
                turn[...] = v.reshape(tall * 8, maps)
                lefts[PASSES] = turn[pl.ds(3, tall, 8), :]

        own = [own_ref[0], own_ref[1], own_ref[2], down_ref[...]]
        strip([left_ref[0], left_ref[1], left_ref[2], dleft_ref[...]], own, -4, True)
        strip(own, [right_ref[0], right_ref[1], right_ref[2], dright_ref[...]], 252, False)

    lane = lax.broadcasted_iota(jnp.int32, (tall, 128), 1)
    at_start, at_end = lane == 0, lane == 127
    b0 = row_bound((tall, 128), 0)
    b1 = jnp.where(first_col + 128 + lane < total_cols - 1, 1.0, 0.0).astype(F32)

    def one(m, _):
        gm = pl.program_id(0) * block + m
        s, u, v = [], [], []
        for c in range(2):
            cols = pl.ds(128 * c, 128)
            d = jnp.concatenate(
                [
                    d_ref[pl.ds(c * maps + gm, rows, 2 * maps), :],
                    drim_ref[pl.ds(c * maps + gm, 8, 2 * maps), :],
                ],
                axis=0,
            )
            s.append(jnp.concatenate([ab_ref[m, :, cols], rim_ref[0, m, :, cols]], axis=0) - 0.1 * d)
            u.append(jnp.clip(jnp.concatenate([q_ref[0, m, :, cols], rim_ref[1, m, :, cols]], axis=0), -b0, b0))
            v.append(jnp.concatenate([q_ref[1, m, :, cols], rim_ref[2, m, :, cols]], axis=0))
        v[1] = jnp.clip(v[1], -b1, b1)

        def field(p):
            edge = pltpu.roll(lefts[p], lax.rem(128 - gm, 128), 1)
            t0, t1 = pltpu.roll(v[0], 1, 1), pltpu.roll(v[1], 1, 1)
            before = [jnp.where(at_start, edge, t0), jnp.where(at_start, t0, t1)]
            return [s[c] - 0.25 * (u[c] - pltpu.roll(u[c], 1, 0) + (v[c] - before[c])) for c in range(2)]

        for p in range(PASSES):
            z = field(p)
            edge = pltpu.roll(rights[p], 127 - gm, 1)
            t0, t1 = pltpu.roll(z[0], 127, 1), pltpu.roll(z[1], 127, 1)
            after = [jnp.where(at_end, t1, t0), jnp.where(at_end, edge, t1)]
            u = [jnp.clip(u[c] + 0.5 * (pltpu.roll(z[c], tall - 1, 0) - z[c]), -b0, b0) for c in range(2)]
            v = [v[c] + 0.5 * (after[c] - z[c]) for c in range(2)]
            v = [jnp.clip(v[0], -1.0, 1.0), jnp.clip(v[1], -b1, b1)]
        z = field(PASSES)
        for c in range(2):
            cols = pl.ds(128 * c, 128)
            abn_ref[m, :, cols] = jnp.maximum(z[c][:rows] - 0.02, 0.0)
            qn_ref[0, m, :, cols] = u[c][:rows]
            qn_ref[1, m, :, cols] = v[c][:rows]
        return 0

    lax.fori_loop(0, block, one, 0)


def tv(origin, abundance, duals, rim, d, drim, strips, dstrips):
    maps, rows, cols = abundance.shape
    block = 8
    tile = pl.BlockSpec((block, rows, cols), lambda i: (i, 0, 0))
    pair = pl.BlockSpec((2, block, rows, cols), lambda i: (0, i, 0, 0))
    rims = pl.BlockSpec((3, block, 8, cols), lambda i: (0, i, 0, 0))
    tall = rows + 8
    return pl.pallas_call(
        tv_kernel,
        grid=(maps // block,),
        out_shape=(
            jax.ShapeDtypeStruct(abundance.shape, F32),
            jax.ShapeDtypeStruct(duals.shape, F32),
        ),
        in_specs=[SCALARS, tile, pair, rims] + [WHOLE] * 8,
        out_specs=(tile, pair),
        scratch_shapes=[
            pltpu.VMEM((PASSES + 1, tall, maps), F32),
            pltpu.VMEM((PASSES, tall, maps), F32),
            pltpu.VMEM((tall * 8, maps), F32),
        ],
        compiler_params=pltpu.CompilerParams(vmem_limit_bytes=LIMIT),
        name="tv",
    )(origin, abundance, duals, rim, d.reshape(-1, 128), drim.reshape(-1, 128), *strips, *dstrips)


def on_device(abundance, duals, reflectance, library):
    maps, height, width = abundance.shape
    y, x = lax.axis_index("lib_0"), lax.axis_index("lib_1")
    share = height // 8
    me = y * 2 + x
    whole_library = lax.all_gather(library, LIB, axis=0, tiled=False)

    compact = abundance.astype(BF16).transpose(1, 0, 2).reshape(8, share, maps, width)
    mine = lax.dynamic_index_in_dim(compact, me, 0, keepdims=False)
    blocks, place = [mine], [me]
    for dy, dx in HOPS:
        to = lax.rem(y + dy, 4) * 2 + (x + dx) % 2
        blocks.append(to_lib(lax.dynamic_index_in_dim(compact, to, 0, keepdims=False), (dy, dx)))
        place.append(lax.rem(y + 4 - dy, 4) * 2 + (x + dx) % 2)
    observed = lax.dynamic_slice_in_dim(reflectance, me * share, share, 1).transpose(1, 0, 2)
    rb = residual(jnp.stack(place), blocks, whole_library, observed)

    state = jnp.concatenate([abundance[None], duals], axis=0)
    first = lax.slice_in_dim(state, 0, 4, axis=2).astype(BF16)
    last = lax.slice_in_dim(state, height - 4, height, axis=2).astype(BF16)
    rim = lax.concatenate([shifted(first, "row", -1), shifted(last, "row", 1)], 2).astype(F32)
    columns = jnp.concatenate([state[..., width - 4 :], state[..., :4]], axis=3)
    strips = strips_two_steps(columns.transpose(0, 2, 3, 1))

    pieces = gathered(rb)
    firsts = [(lax.rem(y + dy, 4) * 2 + (x + dx) % 2) * share + row for _, (dy, dx), row in pieces]
    d = descent(jnp.stack(firsts), [piece for piece, _, _ in pieces], library.T, height)
    d_first, d_last, own = edges(d)
    drim = lax.concatenate([shifted(d_first, "row", -1), shifted(d_last, "row", 1)], 0).astype(F32)
    dstrips = strips_one_step(own)
    origin = jnp.stack(
        [
            lax.axis_index("row") * height,
            lax.axis_index("col") * width,
            height * lax.axis_size("row"),
            width * lax.axis_size("col"),
        ]
    )
    return tv(origin, abundance, duals, rim, d, drim, strips, dstrips)


def solution(mesh):
    torus = Mesh(
        mesh.devices.reshape(4, 2, mesh.shape["row"], mesh.shape["col"]),
        ("lib_0", "lib_1", "row", "col"),
    )
    placed = (P(LIB, "row", "col"), P(None, LIB, "row", "col"), P(None, "row", "col"), P(None, LIB))
    return jax.shard_map(
        on_device,
        mesh=torus,
        in_specs=placed,
        out_specs=(P(LIB, "row", "col"), P(None, LIB, "row", "col")),
        check_vma=False,
    )
```

```python
import functools

import jax
import jax.numpy as jnp
from jax import lax
from jax.experimental import pallas as pl
from jax.experimental.pallas import tpu as pltpu
from jax.sharding import Mesh
from jax.sharding import PartitionSpec as P

PASSES = 3
LIB = ("lib_0", "lib_1")
BF16 = jnp.bfloat16
F32 = jnp.float32
MIB = 1024 * 1024
WHOLE = pl.BlockSpec(memory_space=pltpu.VMEM)
SCALARS = pl.BlockSpec(memory_space=pltpu.SMEM)


def shifted(array, axis, by):
    length = lax.axis_size(axis)
    pairs = [(i, i + by) for i in range(length) if 0 <= i + by < length]
    return lax.ppermute(array, axis, pairs)


def to_all(array):
    return lax.all_to_all(array, LIB, 0, 0, tiled=True)


def tiles_of(array):
    *lead, rows, cols = array.shape
    n = len(lead)
    split = array.reshape(*lead, rows // 8, 8, cols // 128, 128)
    turned = split.transpose(*range(n), n, n + 2, n + 1, n + 3)
    return turned.reshape(*lead, rows // 8, cols // 16, 128)


def outer_columns(halves, lane, spot):
    joined = jnp.where(lane < 64, halves[0], halves[1])
    return pltpu.roll(joined, 4 + 8 * spot, 1)


def columns_of_eight(rows, maps):
    lane = lax.broadcasted_iota(jnp.int32, (maps, 128), 1)
    total = outer_columns(rows(0), lane, 0)
    for j in range(1, 8):
        total = jnp.where(lane // 8 == j, outer_columns(rows(j), lane, j), total)
    return total.T[:64]


def front_kernel(with_compact, *refs):
    in_ref, refs = refs[0], refs[1 if with_compact else 2 :]
    maps = in_ref.shape[-4]
    flat = in_ref.reshape(maps * 16, 128)

    def rows(j):
        return [flat[pl.ds(8 * c + j, maps, 16), :] for c in range(2)]

    if with_compact:
        library, out = refs[0], refs[1]
        share = (out.shape[1] - library.shape[0]) // maps
        for j in range(8):
            for c, half in enumerate(rows(j)):
                out[j // share, pl.ds(j % share * maps, maps), pl.ds(128 * c, 128)] = half.astype(BF16)
        for k in range(8 // share):
            out[k, pl.ds(share * maps, library.shape[0])] = library[...]
    else:
        step = pl.program_id(1)
        for at, out, start in ((0, refs[0], 0), (pl.num_programs(1) - 1, refs[1], 4)):

            @pl.when(step == at)
            def _():
                for j in range(4):
                    for c, half in enumerate(rows(start + j)):
                        out[0, j, :, pl.ds(128 * c, 128)] = half.astype(BF16)

    refs[-1][...] = columns_of_eight(rows, maps).reshape(refs[-1].shape)


def front_abundance(abundance, library):
    maps, height, width = abundance.shape
    share = height // 8
    flat = jnp.concatenate(jnp.split(library, 2), axis=1)
    length = share * maps + flat.shape[0]
    return pl.pallas_call(
        functools.partial(front_kernel, True),
        grid=(height // 8,),
        out_shape=(
            jax.ShapeDtypeStruct((8, length, width), BF16),
            jax.ShapeDtypeStruct((height, 8, maps), F32),
        ),
        in_specs=[pl.BlockSpec((maps, 1, 16, 128), lambda i: (0, i, 0, 0)), WHOLE],
        out_specs=(
            pl.BlockSpec((8 // share, length, width), lambda i: (i, 0, 0)),
            pl.BlockSpec((8, 8, maps), lambda i: (i, 0, 0)),
        ),
        compiler_params=pltpu.CompilerParams(vmem_limit_bytes=56 * MIB),
        name="front_abundance",
    )(tiles_of(abundance), flat)


def front_duals(duals, after):
    _, maps, height, width = duals.shape
    return pl.pallas_call(
        functools.partial(front_kernel, False),
        grid=(2, height // 8),
        out_shape=(
            jax.ShapeDtypeStruct((2, 4, maps, width), BF16),
            jax.ShapeDtypeStruct((2, 4, maps, width), BF16),
            jax.ShapeDtypeStruct((2, height, 8, maps), F32),
        ),
        in_specs=[
            pl.BlockSpec((1, maps, 1, 16, 128), lambda k, i: (k, 0, i, 0, 0)),
            pl.BlockSpec(memory_space=pl.ANY),
        ],
        out_specs=(
            pl.BlockSpec((1, 4, maps, width), lambda k, i: (k, 0, 0, 0)),
            pl.BlockSpec((1, 4, maps, width), lambda k, i: (k, 0, 0, 0)),
            pl.BlockSpec((1, 8, 8, maps), lambda k, i: (k, i, 0, 0)),
        ),
        compiler_params=pltpu.CompilerParams(vmem_limit_bytes=48 * MIB),
        cost_estimate=pl.CostEstimate(flops=0, bytes_accessed=8_000_000, transcendentals=0),
        name="front_duals",
    )(tiles_of(duals), after)


def middle_kernel(blocks, observed, *refs):
    descents = refs[-1]
    parts, share, maps, width = descents.shape
    start = share * maps

    def library(k):
        flat = blocks[k, start:]
        return jnp.concatenate([flat[:, :128], flat[:, 128:]])

    wide = jnp.concatenate([library(k) for k in range(parts)], axis=1)
    tall = jnp.concatenate([library(k).astype(F32).T.astype(BF16) for k in range(parts)])
    for r in range(share):
        pixels = jnp.concatenate([blocks[k, r * maps : r * maps + maps] for k in range(parts)])
        total = jnp.dot(wide, pixels, preferred_element_type=F32) - observed[r].astype(F32)
        d = jnp.dot(tall, total.astype(BF16), preferred_element_type=F32).astype(BF16)
        descents[:, r] = d.reshape(parts, maps, width)


def middle(blocks, observed, maps, first):
    share, _, width = observed.shape
    return pl.pallas_call(
        middle_kernel,
        out_shape=jax.ShapeDtypeStruct((8, share, maps, width), BF16),
        in_specs=[WHOLE] * 2 + [pl.BlockSpec(memory_space=pl.ANY)] * len(first),
        out_specs=WHOLE,
        compiler_params=pltpu.CompilerParams(vmem_limit_bytes=16 * MIB),
        name="middle",
    )(blocks, observed, *first)


def below_then_above(array, dim, reach=4):
    size = array.shape[dim]
    below = shifted(lax.slice_in_dim(array, 0, reach, axis=dim), "row", -1)
    above = shifted(lax.slice_in_dim(array, size - reach, size, axis=dim), "row", 1)
    return lax.concatenate([below, above], dim)


def columns_kernel(in_ref, out_ref):
    fields, rows, maps, _ = in_ref.shape
    for k in range(fields):
        for i in range(rows // 8):

            def pair(j):
                row = in_ref[k, 8 * i + j].astype(F32)
                return [row[:, :128], row[:, 128:]]

            out_ref[k, pl.ds(8 * i, 8)] = columns_of_eight(pair, maps).reshape(8, 8, maps)


def outer_columns_of(array, name):
    fields, rows, maps, _ = array.shape
    return pl.pallas_call(
        columns_kernel,
        out_shape=jax.ShapeDtypeStruct((fields, rows, 8, maps), F32),
        in_specs=[WHOLE],
        out_specs=WHOLE,
        compiler_params=pltpu.CompilerParams(vmem_limit_bytes=8 * MIB),
        name=name,
    )(array)


def beside(columns):
    return columns, shifted(columns, "col", 1), shifted(columns, "col", -1)


def tv_kernel(
    origin,
    ab_ref,
    q_ref,
    rim_ref,
    d_ref,
    drim_ref,
    own_ref,
    left_ref,
    right_ref,
    down_ref,
    dleft_ref,
    dright_ref,
    abn_ref,
    qn_ref,
    lefts,
    rights,
    turn,
):
    block = ab_ref.shape[0]
    rows = d_ref.shape[0]
    tall = rows + 8
    maps = own_ref.shape[-1]
    first_row, first_col, total_rows, total_cols = (origin[i] for i in range(4))

    @pl.when(pl.program_id(0) == 0)
    def _():
        r = lax.broadcasted_iota(jnp.int32, (tall, 8, maps), 0)
        g = first_row + jnp.where(r < rows + 4, r, r - tall)
        b0 = jnp.where((g >= 0) & (g < total_rows - 1), 1.0, 0.0).astype(F32)
        sub = lax.broadcasted_iota(jnp.int32, (tall, 8, maps), 1)

        def keep(out, values, at):
            turn[...] = values.reshape(tall * 8, maps)
            column = turn[pl.ds(at, tall, 8), :]
            out[...] = column

        def strip(nearer, further, dnearer, dfurther, offset, is_left):
            def pick(i):
                return jnp.where(sub < 4, nearer[i], further[i])

            g = first_col + offset + sub
            b1 = jnp.where((g >= 0) & (g < total_cols - 1), 1.0, 0.0).astype(F32)
            s = 0.5 * pick(0) - 0.05 * jnp.where(sub < 4, dnearer[0], dfurther[0])
            u, v = jnp.clip(pick(1), -b0, b0), jnp.clip(pick(2), -b1, b1)
            for p in range(PASSES):
                if is_left:
                    keep(lefts.at[p], v, 3)
                uu = jnp.concatenate([u[tall - 1 :], u[: tall - 1]], axis=0)
                z = s - 0.125 * (u - uu + (v - pltpu.roll(v, 1, 1)))
                if not is_left:
                    keep(rights.at[p], z, 4)
                zd = jnp.concatenate([z[1:], z[:1]], axis=0)
                zr = pltpu.roll(z, 7, 1)
                u = jnp.clip(u + (zd - z), -b0, b0)
                v = jnp.clip(v + (zr - z), -b1, b1)
            if is_left:
                keep(lefts.at[PASSES], v, 3)

        strip(left_ref, own_ref, dleft_ref, down_ref, -4, True)
        strip(own_ref, right_ref, down_ref, dright_ref, 252, False)

    lane = lax.broadcasted_iota(jnp.int32, (tall, 128), 1)
    at_start, at_end = lane == 0, lane == 127
    b1 = jnp.where(first_col + 128 + lane < total_cols - 1, 1.0, 0.0).astype(F32)
    r = lax.broadcasted_iota(jnp.int32, (tall, 128), 0)
    g = first_row + jnp.where(r < rows + 4, r, r - tall)
    b0 = jnp.where((g >= 0) & (g < total_rows - 1), 1.0, 0.0).astype(F32)

    def by_map(ref, c, h):
        cols = pl.ds(128 * c, 128)
        tiles = [
            jnp.swapaxes(ref[pl.ds(8 * i, 8), :, cols].astype(F32)[:, 8 * h : 8 * h + 8], 0, 1)
            for i in range(ref.shape[0] // 8)
        ]
        return tiles[0] if len(tiles) == 1 else jnp.concatenate(tiles, axis=1)

    for h in range(block // 8):
        s, u, v, z = {}, {}, {}, {}
        for c in range(2):
            cols = pl.ds(128 * c, 128)
            d = jnp.concatenate([by_map(d_ref, c, h), by_map(drim_ref, c, h)], axis=1)
            rim = [by_map(rim_ref.at[i], c, h) for i in range(3)]
            for k in range(8):
                m = 8 * h + k
                main = ab_ref[m, :, cols], q_ref[0, m, :, cols], q_ref[1, m, :, cols]
                full = [jnp.concatenate([main[i], rim[i][k]], axis=0) for i in range(3)]
                s[k, c] = 0.5 * full[0] - 0.05 * d[k]
                u[k, c] = jnp.clip(full[1], -b0, b0)
                v[k, c] = jnp.clip(full[2], -b1, b1) if c else full[2]
        gms = [pl.program_id(0) * block + 8 * h + k for k in range(8)]

        def field(p, k):
            edge = pltpu.roll(lefts[p], lax.rem(128 - gms[k], 128), 1)
            t = [pltpu.roll(v[k, c], 1, 1) for c in range(2)]
            before = jnp.where(at_start, edge, t[0]), jnp.where(at_start, t[0], t[1])
            for c in range(2):
                vertical = u[k, c] - pltpu.roll(u[k, c], 1, 0)
                z[k, c] = s[k, c] - 0.125 * (vertical + (v[k, c] - before[c]))

        for p in range(PASSES):
            for k in range(8):
                field(p, k)
            for k in range(8):
                edge = pltpu.roll(rights[p], 127 - gms[k], 1)
                t = [pltpu.roll(z[k, c], 127, 1) for c in range(2)]
                after = jnp.where(at_end, t[1], t[0]), jnp.where(at_end, edge, t[1])
                for c in range(2):
                    below = pltpu.roll(z[k, c], tall - 1, 0)
                    bound = b1 if c else 1.0
                    u[k, c] = jnp.clip(u[k, c] + (below - z[k, c]), -b0, b0)
                    v[k, c] = jnp.clip(v[k, c] + (after[c] - z[k, c]), -bound, bound)
        for k in range(8):
            field(PASSES, k)
            m = 8 * h + k
            for c in range(2):
                cols = pl.ds(128 * c, 128)
                abn_ref[m, :, cols] = jnp.maximum(2.0 * z[k, c][:rows] - 0.02, 0.0)
                qn_ref[0, m, :, cols] = u[k, c][:rows]
                qn_ref[1, m, :, cols] = v[k, c][:rows]


def tv(origin, abundance, duals, rim, d, drim, strips, dstrips):
    maps, rows, cols = abundance.shape
    block = 16
    tall = rows + 8
    tile = pl.BlockSpec((block, rows, cols), lambda i: (i, 0, 0))
    pair = pl.BlockSpec((2, block, rows, cols), lambda i: (0, i, 0, 0))

    def by_row(count):
        return pl.BlockSpec((count, block, cols), lambda i: (0, i, 0))

    return pl.pallas_call(
        tv_kernel,
        grid=(maps // block,),
        out_shape=(
            jax.ShapeDtypeStruct(abundance.shape, F32),
            jax.ShapeDtypeStruct(duals.shape, F32),
        ),
        in_specs=[
            SCALARS,
            tile,
            pair,
            pl.BlockSpec((3, 8, block, cols), lambda i: (0, 0, i, 0)),
            by_row(rows),
            by_row(8),
        ]
        + [WHOLE] * 6,
        out_specs=(tile, pair),
        scratch_shapes=[
            pltpu.VMEM((PASSES + 1, tall, maps), F32),
            pltpu.VMEM((PASSES, tall, maps), F32),
            pltpu.VMEM((tall * 8, maps), F32),
        ],
        compiler_params=pltpu.CompilerParams(vmem_limit_bytes=56 * MIB),
        name="tv",
    )(origin, abundance, duals, rim, d, drim, *strips, *dstrips)


def on_device(abundance, duals, reflectance, library):
    maps, height, width = abundance.shape
    share = height // 8
    me = lax.axis_index(LIB)
    compact, columns = front_abundance(abundance, library)
    blocks = to_all(compact)
    observed = lax.dynamic_slice_in_dim(reflectance, me * share, share, 1).transpose(1, 0, 2)

    first, last, dual_columns = front_duals(duals, compact)
    own = compact[:, : share * maps].reshape(height, maps, width)
    first = jnp.concatenate([own[None, :4], first])
    last = jnp.concatenate([own[None, height - 4 :], last])
    rim = jnp.concatenate([shifted(first, "row", -1), shifted(last, "row", 1)], axis=1)
    columns = jnp.concatenate([columns[None], dual_columns], axis=0)
    strips = beside(jnp.concatenate([columns, outer_columns_of(rim, "rim_columns")], axis=1))

    d = to_all(middle(blocks, observed, maps, [rim]))
    d, strips = lax.optimization_barrier((d, strips))
    d = d.reshape(height, maps, width)
    drim = below_then_above(d, 0)
    dcolumns = outer_columns_of(d[None], "descent_columns")
    dcolumns = jnp.concatenate([dcolumns, outer_columns_of(drim[None], "descent_rim_columns")], axis=1)
    dstrips = beside(dcolumns)
    origin = jnp.stack(
        [
            lax.axis_index("row") * height,
            lax.axis_index("col") * width,
            height * lax.axis_size("row"),
            width * lax.axis_size("col"),
        ]
    )
    return tv(origin, abundance, duals, rim, d, drim, strips, dstrips)


def solution(mesh):
    torus = Mesh(
        mesh.devices.reshape(4, 2, mesh.shape["row"], mesh.shape["col"]),
        ("lib_0", "lib_1", "row", "col"),
    )
    placed = (P(LIB, "row", "col"), P(None, LIB, "row", "col"), P(None, "row", "col"), P(None, LIB))
    return jax.shard_map(
        on_device,
        mesh=torus,
        in_specs=placed,
        out_specs=(P(LIB, "row", "col"), P(None, LIB, "row", "col")),
        check_vma=False,
    )
```

```python
import functools

import jax
import jax.numpy as jnp
from jax import lax
from jax.experimental import pallas as pl
from jax.experimental.pallas import tpu as pltpu
from jax.sharding import Mesh
from jax.sharding import PartitionSpec as P

PASSES = 3
LIB = ("lib_0", "lib_1")
BF16 = jnp.bfloat16
F32 = jnp.float32
MIB = 1024 * 1024
WHOLE = pl.BlockSpec(memory_space=pltpu.VMEM)
SCALARS = pl.BlockSpec(memory_space=pltpu.SMEM)


def shifted(array, axis, by):
    length = lax.axis_size(axis)
    pairs = [(i, i + by) for i in range(length) if 0 <= i + by < length]
    return lax.ppermute(array, axis, pairs)


def to_all(array):
    return lax.all_to_all(array, LIB, 0, 0, tiled=True)


def tiles_of(array):
    *lead, rows, cols = array.shape
    n = len(lead)
    split = array.reshape(*lead, rows // 8, 8, cols // 128, 128)
    turned = split.transpose(*range(n), n, n + 2, n + 1, n + 3)
    return turned.reshape(*lead, rows // 8, cols // 16, 128)


def outer_columns(halves, lane, spot):
    joined = jnp.where(lane < 64, halves[0], halves[1])
    return pltpu.roll(joined, 4 + 8 * spot, 1)


def columns_of_eight(rows, maps):
    lane = lax.broadcasted_iota(jnp.int32, (maps, 128), 1)
    total = outer_columns(rows(0), lane, 0)
    for j in range(1, 8):
        total = jnp.where(lane // 8 == j, outer_columns(rows(j), lane, j), total)
    return total.T[:64]


def front_kernel(with_compact, *refs):
    in_ref, refs = refs[0], refs[1 if with_compact else 2 :]
    maps = in_ref.shape[-4]
    flat = in_ref.reshape(maps * 16, 128)

    def rows(j):
        return [flat[pl.ds(8 * c + j, maps, 16), :] for c in range(2)]

    if with_compact:
        library, out = refs[0], refs[1]
        share = (out.shape[1] - library.shape[0]) // maps
        height = 8 * share
        for j in range(8):
            row = pl.program_id(0) * 8 + j
            inner = jnp.clip(row - 4, 0, height - 9)
            outer = (row < 4) | (row >= height - 4)
            owner = jnp.where(outer, jnp.where(row < 4, row, row - height + 8), inner // (share - 1))
            slot = jnp.where(outer, 0, 1 + inner % (share - 1))
            at = pl.ds(pl.multiple_of(slot * maps, maps), maps)
            for c, half in enumerate(rows(j)):
                out[owner, at, pl.ds(128 * c, 128)] = half.astype(BF16)

        @pl.when(pl.program_id(0) == 0)
        def _():
            for k in range(8):
                out[k, pl.ds(share * maps, library.shape[0])] = library[...]

    else:
        step = pl.program_id(1)
        for at, out, start in ((0, refs[0], 0), (pl.num_programs(1) - 1, refs[1], 4)):

            @pl.when(step == at)
            def _():
                for j in range(4):
                    for c, half in enumerate(rows(start + j)):
                        out[0, j, :, pl.ds(128 * c, 128)] = half.astype(BF16)

    refs[-1][...] = columns_of_eight(rows, maps).reshape(refs[-1].shape)


def front_abundance(abundance, library):
    maps, height, width = abundance.shape
    share = height // 8
    flat = jnp.concatenate(jnp.split(library, 2), axis=1)
    length = share * maps + flat.shape[0]
    return pl.pallas_call(
        functools.partial(front_kernel, True),
        grid=(height // 8,),
        out_shape=(
            jax.ShapeDtypeStruct((8, length, width), BF16),
            jax.ShapeDtypeStruct((height, 8, maps), F32),
        ),
        in_specs=[pl.BlockSpec((maps, 1, 16, 128), lambda i: (0, i, 0, 0)), WHOLE],
        out_specs=(
            pl.BlockSpec((8, length, width), lambda i: (0, 0, 0)),
            pl.BlockSpec((8, 8, maps), lambda i: (i, 0, 0)),
        ),
        compiler_params=pltpu.CompilerParams(vmem_limit_bytes=56 * MIB),
        name="front_abundance",
    )(tiles_of(abundance), flat)


def front_duals(duals, after):
    _, maps, height, width = duals.shape
    return pl.pallas_call(
        functools.partial(front_kernel, False),
        grid=(2, height // 8),
        out_shape=(
            jax.ShapeDtypeStruct((2, 4, maps, width), BF16),
            jax.ShapeDtypeStruct((2, 4, maps, width), BF16),
            jax.ShapeDtypeStruct((2, height, 8, maps), F32),
        ),
        in_specs=[
            pl.BlockSpec((1, maps, 1, 16, 128), lambda k, i: (k, 0, i, 0, 0)),
            pl.BlockSpec(memory_space=pl.ANY),
        ],
        out_specs=(
            pl.BlockSpec((1, 4, maps, width), lambda k, i: (k, 0, 0, 0)),
            pl.BlockSpec((1, 4, maps, width), lambda k, i: (k, 0, 0, 0)),
            pl.BlockSpec((1, 8, 8, maps), lambda k, i: (k, i, 0, 0)),
        ),
        compiler_params=pltpu.CompilerParams(vmem_limit_bytes=48 * MIB),
        cost_estimate=pl.CostEstimate(flops=0, bytes_accessed=8_000_000, transcendentals=0),
        name="front_duals",
    )(tiles_of(duals), after)


def middle_kernel(blocks, observed, *refs):
    outer, inner = refs[-2:]
    parts, more, maps, width = inner.shape
    share, bands, _ = observed.shape
    start = share * maps
    lane = lax.broadcasted_iota(jnp.int32, (bands, 128), 1)

    def library(k):
        flat = blocks[k, start:]
        return jnp.concatenate([flat[:, :128], flat[:, 128:]])

    wide = jnp.concatenate([library(k) for k in range(parts)], axis=1)
    tall = jnp.concatenate([library(k).astype(F32).T.astype(BF16) for k in range(parts)])
    packed = jnp.zeros((bands, 128), F32)
    for r in range(share):
        pixels = jnp.concatenate([blocks[k, r * maps : r * maps + maps] for k in range(parts)])
        total = jnp.dot(wide, pixels, preferred_element_type=F32) - observed[r].astype(F32)
        rb = total.astype(BF16)
        d = jnp.dot(tall, rb, preferred_element_type=F32).astype(BF16).reshape(parts, maps, width)
        if r == 0:
            outer[:, :maps] = d
        else:
            inner[:, r - 1] = d
        exact = rb.astype(F32)
        moved = outer_columns([exact[:, :128], exact[:, 128:]], lane, r)
        packed = jnp.where(lane // 8 == r, moved, packed)
    columns = packed.T[: 8 * share].astype(BF16)
    d = jnp.dot(columns, wide, preferred_element_type=F32).astype(BF16)
    half = 4 * share
    for k in range(parts):
        for c in range(2):
            piece = d[half * c : half * c + half, k * maps : k * maps + maps]
            outer[k, pl.ds(maps, half), pl.ds(128 * c, 128)] = piece


def middle(blocks, observed, maps, first):
    share, _, width = observed.shape
    return pl.pallas_call(
        middle_kernel,
        out_shape=(
            jax.ShapeDtypeStruct((8, maps + 4 * share, width), BF16),
            jax.ShapeDtypeStruct((8, share - 1, maps, width), BF16),
        ),
        in_specs=[WHOLE] * 2 + [pl.BlockSpec(memory_space=pl.ANY)] * len(first),
        out_specs=(WHOLE, WHOLE),
        compiler_params=pltpu.CompilerParams(vmem_limit_bytes=16 * MIB),
        name="middle",
    )(blocks, observed, *first)


def below_then_above(array, dim, reach=4):
    size = array.shape[dim]
    below = shifted(lax.slice_in_dim(array, 0, reach, axis=dim), "row", -1)
    above = shifted(lax.slice_in_dim(array, size - reach, size, axis=dim), "row", 1)
    return lax.concatenate([below, above], dim)


def columns_kernel(in_ref, out_ref):
    fields, rows, maps, _ = in_ref.shape
    for k in range(fields):
        for i in range(rows // 8):

            def pair(j):
                row = in_ref[k, 8 * i + j].astype(F32)
                return [row[:, :128], row[:, 128:]]

            out_ref[k, pl.ds(8 * i, 8)] = columns_of_eight(pair, maps).reshape(8, 8, maps)


def outer_columns_of(array, name):
    fields, rows, maps, _ = array.shape
    return pl.pallas_call(
        columns_kernel,
        out_shape=jax.ShapeDtypeStruct((fields, rows, 8, maps), F32),
        in_specs=[WHOLE],
        out_specs=WHOLE,
        compiler_params=pltpu.CompilerParams(vmem_limit_bytes=8 * MIB),
        name=name,
    )(array)


def beside(columns):
    return columns, shifted(columns, "col", 1), shifted(columns, "col", -1)


def tv_kernel(
    origin,
    ab_ref,
    q_ref,
    rim_ref,
    douter_ref,
    dinner_ref,
    drim_ref,
    own_ref,
    left_ref,
    right_ref,
    down_ref,
    dleft_ref,
    dright_ref,
    abn_ref,
    qn_ref,
    lefts,
    rights,
    turn,
):
    block = ab_ref.shape[0]
    rows = ab_ref.shape[1]
    tall = rows + 8
    maps = own_ref.shape[-1]
    first_row, first_col, total_rows, total_cols = (origin[i] for i in range(4))

    @pl.when(pl.program_id(0) == 0)
    def _():
        r = lax.broadcasted_iota(jnp.int32, (tall, 8, maps), 0)
        g = first_row + jnp.where(r < rows + 4, r, r - tall)
        b0 = jnp.where((g >= 0) & (g < total_rows - 1), 1.0, 0.0).astype(F32)
        sub = lax.broadcasted_iota(jnp.int32, (tall, 8, maps), 1)

        def keep(out, values, at):
            turn[...] = values.reshape(tall * 8, maps)
            column = turn[pl.ds(at, tall, 8), :]
            out[...] = column

        def strip(nearer, further, dnearer, dfurther, offset, is_left):
            def pick(i):
                return jnp.where(sub < 4, nearer[i], further[i])

            g = first_col + offset + sub
            b1 = jnp.where((g >= 0) & (g < total_cols - 1), 1.0, 0.0).astype(F32)
            s = 0.5 * pick(0) - 0.05 * jnp.where(sub < 4, dnearer[0], dfurther[0])
            u, v = jnp.clip(pick(1), -b0, b0), jnp.clip(pick(2), -b1, b1)
            for p in range(PASSES):
                if is_left:
                    keep(lefts.at[p], v, 3)
                uu = jnp.concatenate([u[tall - 1 :], u[: tall - 1]], axis=0)
                z = s - 0.125 * (u - uu + (v - pltpu.roll(v, 1, 1)))
                if not is_left:
                    keep(rights.at[p], z, 4)
                zd = jnp.concatenate([z[1:], z[:1]], axis=0)
                zr = pltpu.roll(z, 7, 1)
                u = jnp.clip(u + (zd - z), -b0, b0)
                v = jnp.clip(v + (zr - z), -b1, b1)
            if is_left:
                keep(lefts.at[PASSES], v, 3)

        strip(left_ref, own_ref, dleft_ref, down_ref, -4, True)
        strip(own_ref, right_ref, down_ref, dright_ref, 252, False)

    lane = lax.broadcasted_iota(jnp.int32, (tall, 128), 1)
    at_start, at_end = lane == 0, lane == 127
    b1 = jnp.where(first_col + 128 + lane < total_cols - 1, 1.0, 0.0).astype(F32)
    r = lax.broadcasted_iota(jnp.int32, (tall, 128), 0)
    g = first_row + jnp.where(r < rows + 4, r, r - tall)
    b0 = jnp.where((g >= 0) & (g < total_rows - 1), 1.0, 0.0).astype(F32)

    def by_map(c, h, *pieces):
        cols = pl.ds(128 * c, 128)
        found = [ref[pl.ds(at, n), :, cols].astype(F32)[:, 8 * h : 8 * h + 8] for ref, at, n in pieces]
        return jnp.swapaxes(found[0] if len(found) == 1 else jnp.concatenate(found), 0, 1)

    inner = rows - 8
    descents = [[(douter_ref, 0, 4), (dinner_ref, 0, 4)]]
    descents += [[(dinner_ref, at, 8)] for at in range(4, inner - 4, 8)]
    descents += [[(dinner_ref, inner - 4, 4), (douter_ref, 4, 4)], [(drim_ref, 0, 8)]]

    for h in range(block // 8):
        s, u, v, z = {}, {}, {}, {}
        for c in range(2):
            cols = pl.ds(128 * c, 128)
            d = jnp.concatenate([by_map(c, h, *pieces) for pieces in descents], axis=1)
            rim = [by_map(c, h, (rim_ref.at[i], 0, 8)) for i in range(3)]
            for k in range(8):
                m = 8 * h + k
                main = ab_ref[m, :, cols], q_ref[0, m, :, cols], q_ref[1, m, :, cols]
                full = [jnp.concatenate([main[i], rim[i][k]], axis=0) for i in range(3)]
                s[k, c] = 0.5 * full[0] - 0.05 * d[k]
                u[k, c] = jnp.clip(full[1], -b0, b0)
                v[k, c] = jnp.clip(full[2], -b1, b1) if c else full[2]
        gms = [pl.program_id(0) * block + 8 * h + k for k in range(8)]

        def field(p, k):
            edge = pltpu.roll(lefts[p], lax.rem(128 - gms[k], 128), 1)
            t = [pltpu.roll(v[k, c], 1, 1) for c in range(2)]
            before = jnp.where(at_start, edge, t[0]), jnp.where(at_start, t[0], t[1])
            for c in range(2):
                vertical = u[k, c] - pltpu.roll(u[k, c], 1, 0)
                z[k, c] = s[k, c] - 0.125 * (vertical + (v[k, c] - before[c]))

        for p in range(PASSES):
            for k in range(8):
                field(p, k)
            for k in range(8):
                edge = pltpu.roll(rights[p], 127 - gms[k], 1)
                t = [pltpu.roll(z[k, c], 127, 1) for c in range(2)]
                after = jnp.where(at_end, t[1], t[0]), jnp.where(at_end, edge, t[1])
                for c in range(2):
                    below = pltpu.roll(z[k, c], tall - 1, 0)
                    bound = b1 if c else 1.0
                    u[k, c] = jnp.clip(u[k, c] + (below - z[k, c]), -b0, b0)
                    v[k, c] = jnp.clip(v[k, c] + (after[c] - z[k, c]), -bound, bound)
        for k in range(8):
            field(PASSES, k)
            m = 8 * h + k
            for c in range(2):
                cols = pl.ds(128 * c, 128)
                abn_ref[m, :, cols] = jnp.maximum(2.0 * z[k, c][:rows] - 0.02, 0.0)
                qn_ref[0, m, :, cols] = u[k, c][:rows]
                qn_ref[1, m, :, cols] = v[k, c][:rows]


def tv(origin, abundance, duals, rim, douter, dinner, drim, strips, dstrips):
    maps, rows, cols = abundance.shape
    block = 16
    tall = rows + 8
    tile = pl.BlockSpec((block, rows, cols), lambda i: (i, 0, 0))
    pair = pl.BlockSpec((2, block, rows, cols), lambda i: (0, i, 0, 0))

    def by_row(count):
        return pl.BlockSpec((count, block, cols), lambda i: (0, i, 0))

    return pl.pallas_call(
        tv_kernel,
        grid=(maps // block,),
        out_shape=(
            jax.ShapeDtypeStruct(abundance.shape, F32),
            jax.ShapeDtypeStruct(duals.shape, F32),
        ),
        in_specs=[
            SCALARS,
            tile,
            pair,
            pl.BlockSpec((3, 8, block, cols), lambda i: (0, 0, i, 0)),
            by_row(8),
            by_row(rows - 8),
            by_row(8),
        ]
        + [WHOLE] * 6,
        out_specs=(tile, pair),
        scratch_shapes=[
            pltpu.VMEM((PASSES + 1, tall, maps), F32),
            pltpu.VMEM((PASSES, tall, maps), F32),
            pltpu.VMEM((tall * 8, maps), F32),
        ],
        compiler_params=pltpu.CompilerParams(vmem_limit_bytes=56 * MIB),
        name="tv",
    )(origin, abundance, duals, rim, douter, dinner, drim, *strips, *dstrips)


def on_device(abundance, duals, reflectance, library):
    maps, height, width = abundance.shape
    share = height // 8
    me = lax.axis_index(LIB)
    compact, columns = front_abundance(abundance, library)
    blocks = to_all(compact)
    outer_row = jnp.where(me < 4, me, me + height - 8)
    observed = [
        lax.dynamic_slice_in_dim(reflectance, outer_row, 1, 1),
        lax.dynamic_slice_in_dim(reflectance, 4 + me * (share - 1), share - 1, 1),
    ]
    observed = jnp.concatenate(observed, axis=1).transpose(1, 0, 2)

    first, last, dual_columns = front_duals(duals, compact)
    first = jnp.concatenate([compact[None, :4, :maps], first])
    last = jnp.concatenate([compact[None, 4:, :maps], last])
    rim = jnp.concatenate([shifted(first, "row", -1), shifted(last, "row", 1)], axis=1)
    columns = jnp.concatenate([columns[None], dual_columns], axis=0)
    strips = beside(jnp.concatenate([columns, outer_columns_of(rim, "rim_columns")], axis=1))

    outer, inner = middle(blocks, observed, maps, [rim])
    outer = to_all(outer)
    inner, outer, strips = lax.optimization_barrier((inner, outer, strips))
    dinner = to_all(inner).reshape(height - 8, maps, width)
    douter = outer[:, :maps]
    sides = [half.reshape(8, share // 2, 8, maps) for half in jnp.split(outer[:, maps:], 2, axis=2)]
    sides = jnp.concatenate(sides, axis=1).astype(F32)
    middle_rows = sides[:, 1:].reshape(height - 8, 8, maps)
    drim = below_then_above(douter, 0)
    above = outer_columns_of(drim[None], "descent_rim_columns")[0]
    dstrips = beside(jnp.concatenate([sides[:4, 0], middle_rows, sides[4:, 0], above])[None])
    origin = jnp.stack(
        [
            lax.axis_index("row") * height,
            lax.axis_index("col") * width,
            height * lax.axis_size("row"),
            width * lax.axis_size("col"),
        ]
    )
    return tv(origin, abundance, duals, rim, douter, dinner, drim, strips, dstrips)


def solution(mesh):
    torus = Mesh(
        mesh.devices.reshape(4, 2, mesh.shape["row"], mesh.shape["col"]),
        ("lib_0", "lib_1", "row", "col"),
    )
    placed = (P(LIB, "row", "col"), P(None, LIB, "row", "col"), P(None, "row", "col"), P(None, LIB))
    return jax.shard_map(
        on_device,
        mesh=torus,
        in_specs=placed,
        out_specs=(P(LIB, "row", "col"), P(None, LIB, "row", "col")),
        check_vma=False,
    )
```

```python
import functools

import jax
import jax.numpy as jnp
from jax import lax
from jax.experimental import pallas as pl
from jax.experimental.pallas import tpu as pltpu
from jax.sharding import Mesh
from jax.sharding import PartitionSpec as P

PASSES = 3
LIB = ("lib_0", "lib_1")
BF16 = jnp.bfloat16
F32 = jnp.float32
MIB = 1024 * 1024
WHOLE = pl.BlockSpec(memory_space=pltpu.VMEM)
SCALARS = pl.BlockSpec(memory_space=pltpu.SMEM)


def shifted(array, axis, by):
    length = lax.axis_size(axis)
    pairs = [(i, i + by) for i in range(length) if 0 <= i + by < length]
    return lax.ppermute(array, axis, pairs)


def to_all(array):
    return lax.all_to_all(array, LIB, 0, 0, tiled=True)


def tiles_of(array):
    *lead, rows, cols = array.shape
    n = len(lead)
    split = array.reshape(*lead, rows // 8, 8, cols // 128, 128)
    turned = split.transpose(*range(n), n, n + 2, n + 1, n + 3)
    return turned.reshape(*lead, rows // 8, cols // 16, 128)


def outer_columns(halves, lane, spot):
    joined = jnp.where(lane < 64, halves[0], halves[1])
    return pltpu.roll(joined, 4 + 8 * spot, 1)


def columns_of_eight(rows, maps):
    lane = lax.broadcasted_iota(jnp.int32, (maps, 128), 1)
    total = outer_columns(rows(0), lane, 0)
    for j in range(1, 8):
        total = jnp.where(lane // 8 == j, outer_columns(rows(j), lane, j), total)
    return total.T[:64]


def front_kernel(with_compact, *refs):
    in_ref, by_row, refs = refs[0], refs[-1], refs[1 if with_compact else 2 : -1]
    in_ref = in_ref if with_compact else in_ref.at[0]
    maps = in_ref.shape[0]
    for at in range(0, maps, 8):
        for c in range(2):
            tile = jnp.swapaxes(in_ref[at : at + 8, 0, 8 * c : 8 * c + 8, :], 0, 1)
            by_row[:, at : at + 8, 128 * c : 128 * c + 128] = tile

    def rows(j):
        return [by_row[j, :, 128 * c : 128 * c + 128] for c in range(2)]

    if with_compact:
        library, out = refs[0], refs[1]
        share = (out.shape[1] - library.shape[0] // 2) // maps
        height = 8 * share
        for j in range(8):
            row = pl.program_id(0) * 8 + j
            inner = jnp.clip(row - 4, 0, height - 9)
            outer = (row < 4) | (row >= height - 4)
            owner = jnp.where(outer, jnp.where(row < 4, row, row - height + 8), inner // (share - 1))
            slot = jnp.where(outer, 0, 1 + inner % (share - 1))
            at = pl.ds(pl.multiple_of(slot * maps, maps), maps)
            for c, half in enumerate(rows(j)):
                out[owner, at, pl.ds(128 * c, 128)] = half.astype(BF16)

        @pl.when(pl.program_id(0) == 0)
        def _():
            half = library.shape[0] // 2
            for k in range(8):
                for c in range(2):
                    piece = library[half * c : half * c + half]
                    out[k, pl.ds(share * maps, half), pl.ds(128 * c, 128)] = piece

    else:
        step = pl.program_id(1)
        for at, out, start in ((0, refs[0], 0), (pl.num_programs(1) - 1, refs[1], 4)):

            @pl.when(step == at)
            def _():
                for j in range(4):
                    for c, half in enumerate(rows(start + j)):
                        out[0, j, :, pl.ds(128 * c, 128)] = half.astype(BF16)

    refs[-1][...] = columns_of_eight(rows, maps).reshape(refs[-1].shape)


def front_abundance(abundance, library):
    maps, height, width = abundance.shape
    share = height // 8
    length = share * maps + library.shape[0] // 2
    return pl.pallas_call(
        functools.partial(front_kernel, True),
        grid=(height // 8,),
        out_shape=(
            jax.ShapeDtypeStruct((8, length, width), BF16),
            jax.ShapeDtypeStruct((height, 8, maps), F32),
        ),
        in_specs=[pl.BlockSpec((maps, 1, 16, 128), lambda i: (0, i, 0, 0)), WHOLE],
        out_specs=(
            pl.BlockSpec((8, length, width), lambda i: (0, 0, 0)),
            pl.BlockSpec((8, 8, maps), lambda i: (i, 0, 0)),
        ),
        scratch_shapes=[pltpu.VMEM((8, maps, width), F32)],
        compiler_params=pltpu.CompilerParams(vmem_limit_bytes=56 * MIB),
        name="front_abundance",
    )(tiles_of(abundance), library)


def front_duals(duals, after):
    _, maps, height, width = duals.shape
    return pl.pallas_call(
        functools.partial(front_kernel, False),
        grid=(2, height // 8),
        out_shape=(
            jax.ShapeDtypeStruct((2, 4, maps, width), BF16),
            jax.ShapeDtypeStruct((2, 4, maps, width), BF16),
            jax.ShapeDtypeStruct((2, height, 8, maps), F32),
        ),
        in_specs=[
            pl.BlockSpec((1, maps, 1, 16, 128), lambda k, i: (k, 0, i, 0, 0)),
            pl.BlockSpec(memory_space=pl.ANY),
        ],
        out_specs=(
            pl.BlockSpec((1, 4, maps, width), lambda k, i: (k, 0, 0, 0)),
            pl.BlockSpec((1, 4, maps, width), lambda k, i: (k, 0, 0, 0)),
            pl.BlockSpec((1, 8, 8, maps), lambda k, i: (k, i, 0, 0)),
        ),
        scratch_shapes=[pltpu.VMEM((8, maps, width), F32)],
        compiler_params=pltpu.CompilerParams(vmem_limit_bytes=48 * MIB),
        cost_estimate=pl.CostEstimate(flops=0, bytes_accessed=8_000_000, transcendentals=0),
        name="front_duals",
    )(tiles_of(duals), after)


def middle_kernel(blocks, observed, *refs):
    outer, inner = refs[-2:]
    parts, more, maps, width = inner.shape
    share, bands, _ = observed.shape
    start = share * maps
    lane = lax.broadcasted_iota(jnp.int32, (bands, 128), 1)

    def library(k):
        flat = blocks[k, start:]
        return jnp.concatenate([flat[:, :128], flat[:, 128:]])

    wide = jnp.concatenate([library(k) for k in range(parts)], axis=1)
    tall = jnp.concatenate([library(k).astype(F32).T.astype(BF16) for k in range(parts)])
    packed = jnp.zeros((bands, 128), F32)
    for r in range(share):
        pixels = jnp.concatenate([blocks[k, r * maps : r * maps + maps] for k in range(parts)])
        total = jnp.dot(wide, pixels, preferred_element_type=F32) - observed[r].astype(F32)
        rb = total.astype(BF16)
        d = jnp.dot(tall, rb, preferred_element_type=F32).astype(BF16).reshape(parts, maps, width)
        if r == 0:
            outer[:, :maps] = d
        else:
            inner[:, r - 1] = d
        exact = rb.astype(F32)
        moved = outer_columns([exact[:, :128], exact[:, 128:]], lane, r)
        packed = jnp.where(lane // 8 == r, moved, packed)
    columns = packed.T[: 8 * share].astype(BF16)
    d = jnp.dot(columns, wide, preferred_element_type=F32).astype(BF16)
    half = 4 * share
    for k in range(parts):
        for c in range(2):
            piece = d[half * c : half * c + half, k * maps : k * maps + maps]
            outer[k, pl.ds(maps, half), pl.ds(128 * c, 128)] = piece


def middle(blocks, observed, maps, first):
    share, _, width = observed.shape
    return pl.pallas_call(
        middle_kernel,
        out_shape=(
            jax.ShapeDtypeStruct((8, maps + 4 * share, width), BF16),
            jax.ShapeDtypeStruct((8, share - 1, maps, width), BF16),
        ),
        in_specs=[WHOLE] * 2 + [pl.BlockSpec(memory_space=pl.ANY)] * len(first),
        out_specs=(WHOLE, WHOLE),
        compiler_params=pltpu.CompilerParams(vmem_limit_bytes=16 * MIB),
        name="middle",
    )(blocks, observed, *first)


def below_then_above(array, dim, reach=4):
    size = array.shape[dim]
    below = shifted(lax.slice_in_dim(array, 0, reach, axis=dim), "row", -1)
    above = shifted(lax.slice_in_dim(array, size - reach, size, axis=dim), "row", 1)
    return lax.concatenate([below, above], dim)


def columns_kernel(in_ref, out_ref):
    fields, rows, maps, _ = in_ref.shape
    for k in range(fields):
        for i in range(rows // 8):

            def pair(j):
                row = in_ref[k, 8 * i + j].astype(F32)
                return [row[:, :128], row[:, 128:]]

            out_ref[k, pl.ds(8 * i, 8)] = columns_of_eight(pair, maps).reshape(8, 8, maps)


def outer_columns_of(array, name):
    fields, rows, maps, _ = array.shape
    return pl.pallas_call(
        columns_kernel,
        out_shape=jax.ShapeDtypeStruct((fields, rows, 8, maps), F32),
        in_specs=[WHOLE],
        out_specs=WHOLE,
        compiler_params=pltpu.CompilerParams(vmem_limit_bytes=8 * MIB),
        name=name,
    )(array)


def beside(columns):
    return columns, shifted(columns, "col", 1), shifted(columns, "col", -1)


def tv_kernel(
    origin,
    ab_ref,
    q_ref,
    rim_ref,
    douter_ref,
    dinner_ref,
    drim_ref,
    own_ref,
    left_ref,
    right_ref,
    down_ref,
    dleft_ref,
    dright_ref,
    abn_ref,
    qn_ref,
    lefts,
    rights,
    turn,
):
    block = ab_ref.shape[0]
    rows = ab_ref.shape[1]
    tall = rows + 8
    maps = own_ref.shape[-1]
    first_row, first_col, total_rows, total_cols = (origin[i] for i in range(4))

    @pl.when(pl.program_id(0) == 0)
    def _():
        r = lax.broadcasted_iota(jnp.int32, (tall, 8, maps), 0)
        g = first_row + jnp.where(r < rows + 4, r, r - tall)
        b0 = jnp.where((g >= 0) & (g < total_rows - 1), 1.0, 0.0).astype(F32)
        sub = lax.broadcasted_iota(jnp.int32, (tall, 8, maps), 1)

        def keep(out, values, at):
            turn[...] = values.reshape(tall * 8, maps)
            column = turn[pl.ds(at, tall, 8), :]
            out[...] = column

        def strip(nearer, further, dnearer, dfurther, offset, is_left):
            def pick(i):
                return jnp.where(sub < 4, nearer[i], further[i])

            g = first_col + offset + sub
            b1 = jnp.where((g >= 0) & (g < total_cols - 1), 1.0, 0.0).astype(F32)
            s = 0.5 * pick(0) - 0.05 * jnp.where(sub < 4, dnearer[0], dfurther[0])
            u, v = jnp.clip(pick(1), -b0, b0), jnp.clip(pick(2), -b1, b1)
            for p in range(PASSES):
                if is_left:
                    keep(lefts.at[p], v, 3)
                uu = jnp.concatenate([u[tall - 1 :], u[: tall - 1]], axis=0)
                z = s - 0.125 * (u - uu + (v - pltpu.roll(v, 1, 1)))
                if not is_left:
                    keep(rights.at[p], z, 4)
                zd = jnp.concatenate([z[1:], z[:1]], axis=0)
                zr = pltpu.roll(z, 7, 1)
                u = jnp.clip(u + (zd - z), -b0, b0)
                v = jnp.clip(v + (zr - z), -b1, b1)
            if is_left:
                keep(lefts.at[PASSES], v, 3)

        strip(left_ref, own_ref, dleft_ref, down_ref, -4, True)
        strip(own_ref, right_ref, down_ref, dright_ref, 252, False)

    lane = lax.broadcasted_iota(jnp.int32, (tall, 128), 1)
    at_start, at_end = lane == 0, lane == 127
    b1 = jnp.where(first_col + 128 + lane < total_cols - 1, 1.0, 0.0).astype(F32)
    r = lax.broadcasted_iota(jnp.int32, (tall, 128), 0)
    g = first_row + jnp.where(r < rows + 4, r, r - tall)
    b0 = jnp.where((g >= 0) & (g < total_rows - 1), 1.0, 0.0).astype(F32)

    def by_map(c, h, *pieces):
        cols = pl.ds(128 * c, 128)
        found = [ref[pl.ds(at, n), :, cols].astype(F32)[:, 8 * h : 8 * h + 8] for ref, at, n in pieces]
        return jnp.swapaxes(found[0] if len(found) == 1 else jnp.concatenate(found), 0, 1)

    inner = rows - 8
    descents = [[(douter_ref, 0, 4), (dinner_ref, 0, 4)]]
    descents += [[(dinner_ref, at, 8)] for at in range(4, inner - 4, 8)]
    descents += [[(dinner_ref, inner - 4, 4), (douter_ref, 4, 4)], [(drim_ref, 0, 8)]]

    for h in range(block // 8):
        s, u, v, z = {}, {}, {}, {}
        for c in range(2):
            cols = pl.ds(128 * c, 128)
            d = jnp.concatenate([by_map(c, h, *pieces) for pieces in descents], axis=1)
            rim = [by_map(c, h, (rim_ref.at[i], 0, 8)) for i in range(3)]
            for k in range(8):
                m = 8 * h + k
                main = ab_ref[m, :, cols], q_ref[0, m, :, cols], q_ref[1, m, :, cols]
                full = [jnp.concatenate([main[i], rim[i][k]], axis=0) for i in range(3)]
                s[k, c] = 0.5 * full[0] - 0.05 * d[k]
                u[k, c] = jnp.clip(full[1], -b0, b0)
                v[k, c] = jnp.clip(full[2], -b1, b1) if c else full[2]
        gms = [pl.program_id(0) * block + 8 * h + k for k in range(8)]

        def field(p, k):
            edge = pltpu.roll(lefts[p], lax.rem(128 - gms[k], 128), 1)
            t = [pltpu.roll(v[k, c], 1, 1) for c in range(2)]
            before = jnp.where(at_start, edge, t[0]), jnp.where(at_start, t[0], t[1])
            for c in range(2):
                vertical = u[k, c] - pltpu.roll(u[k, c], 1, 0)
                z[k, c] = s[k, c] - 0.125 * (vertical + (v[k, c] - before[c]))

        for p in range(PASSES):
            for k in range(8):
                field(p, k)
            for k in range(8):
                edge = pltpu.roll(rights[p], 127 - gms[k], 1)
                t = [pltpu.roll(z[k, c], 127, 1) for c in range(2)]
                after = jnp.where(at_end, t[1], t[0]), jnp.where(at_end, edge, t[1])
                for c in range(2):
                    below = pltpu.roll(z[k, c], tall - 1, 0)
                    bound = b1 if c else 1.0
                    u[k, c] = jnp.clip(u[k, c] + (below - z[k, c]), -b0, b0)
                    v[k, c] = jnp.clip(v[k, c] + (after[c] - z[k, c]), -bound, bound)
        for k in range(8):
            field(PASSES, k)
            m = 8 * h + k
            for c in range(2):
                cols = pl.ds(128 * c, 128)
                abn_ref[m, :, cols] = jnp.maximum(2.0 * z[k, c][:rows] - 0.02, 0.0)
                qn_ref[0, m, :, cols] = u[k, c][:rows]
                qn_ref[1, m, :, cols] = v[k, c][:rows]


def tv(origin, abundance, duals, rim, douter, dinner, drim, strips, dstrips):
    maps, rows, cols = abundance.shape
    block = 16
    tall = rows + 8
    tile = pl.BlockSpec((block, rows, cols), lambda i: (i, 0, 0))
    pair = pl.BlockSpec((2, block, rows, cols), lambda i: (0, i, 0, 0))

    def by_row(count):
        return pl.BlockSpec((count, block, cols), lambda i: (0, i, 0))

    return pl.pallas_call(
        tv_kernel,
        grid=(maps // block,),
        out_shape=(
            jax.ShapeDtypeStruct(abundance.shape, F32),
            jax.ShapeDtypeStruct(duals.shape, F32),
        ),
        in_specs=[
            SCALARS,
            tile,
            pair,
            pl.BlockSpec((3, 8, block, cols), lambda i: (0, 0, i, 0)),
            by_row(8),
            by_row(rows - 8),
            by_row(8),
        ]
        + [WHOLE] * 6,
        out_specs=(tile, pair),
        scratch_shapes=[
            pltpu.VMEM((PASSES + 1, tall, maps), F32),
            pltpu.VMEM((PASSES, tall, maps), F32),
            pltpu.VMEM((tall * 8, maps), F32),
        ],
        compiler_params=pltpu.CompilerParams(vmem_limit_bytes=56 * MIB),
        name="tv",
    )(origin, abundance, duals, rim, douter, dinner, drim, *strips, *dstrips)


def on_device(abundance, duals, reflectance, library):
    maps, height, width = abundance.shape
    share = height // 8
    me = lax.axis_index(LIB)
    compact, columns = front_abundance(abundance, library)
    blocks = to_all(compact)
    outer_row = jnp.where(me < 4, me, me + height - 8)
    observed = [
        lax.dynamic_slice_in_dim(reflectance, outer_row, 1, 1),
        lax.dynamic_slice_in_dim(reflectance, 4 + me * (share - 1), share - 1, 1),
    ]
    observed = jnp.concatenate(observed, axis=1).transpose(1, 0, 2)

    first, last, dual_columns = front_duals(duals, compact)
    first = jnp.concatenate([compact[None, :4, :maps], first])
    last = jnp.concatenate([compact[None, 4:, :maps], last])
    rim = jnp.concatenate([shifted(first, "row", -1), shifted(last, "row", 1)], axis=1)
    columns = jnp.concatenate([columns[None], dual_columns], axis=0)
    strips = beside(jnp.concatenate([columns, outer_columns_of(rim, "rim_columns")], axis=1))

    outer, inner = middle(blocks, observed, maps, [rim])
    outer = to_all(outer)
    inner, outer, strips = lax.optimization_barrier((inner, outer, strips))
    dinner = to_all(inner).reshape(height - 8, maps, width)
    douter = outer[:, :maps]
    sides = [half.reshape(8, share // 2, 8, maps) for half in jnp.split(outer[:, maps:], 2, axis=2)]
    sides = jnp.concatenate(sides, axis=1).astype(F32)
    middle_rows = sides[:, 1:].reshape(height - 8, 8, maps)
    drim = below_then_above(douter, 0)
    above = outer_columns_of(drim[None], "descent_rim_columns")[0]
    dstrips = beside(jnp.concatenate([sides[:4, 0], middle_rows, sides[4:, 0], above])[None])
    origin = jnp.stack(
        [
            lax.axis_index("row") * height,
            lax.axis_index("col") * width,
            height * lax.axis_size("row"),
            width * lax.axis_size("col"),
        ]
    )
    return tv(origin, abundance, duals, rim, douter, dinner, drim, strips, dstrips)


def solution(mesh):
    torus = Mesh(
        mesh.devices.reshape(4, 2, mesh.shape["row"], mesh.shape["col"]),
        ("lib_0", "lib_1", "row", "col"),
    )
    placed = (P(LIB, "row", "col"), P(None, LIB, "row", "col"), P(None, "row", "col"), P(None, LIB))
    return jax.shard_map(
        on_device,
        mesh=torus,
        in_specs=placed,
        out_specs=(P(LIB, "row", "col"), P(None, LIB, "row", "col")),
        check_vma=False,
    )
```

```python
import functools

import jax
import jax.numpy as jnp
from jax import lax
from jax.experimental import pallas as pl
from jax.experimental.pallas import tpu as pltpu
from jax.sharding import Mesh
from jax.sharding import PartitionSpec as P

PASSES = 3
LIB = ("lib_0", "lib_1")
BF16 = jnp.bfloat16
F32 = jnp.float32
MIB = 1024 * 1024
WHOLE = pl.BlockSpec(memory_space=pltpu.VMEM)
SCALARS = pl.BlockSpec(memory_space=pltpu.SMEM)


def shifted(array, axis, by):
    length = lax.axis_size(axis)
    pairs = [(i, i + by) for i in range(length) if 0 <= i + by < length]
    return lax.ppermute(array, axis, pairs)


def to_all(array):
    return lax.all_to_all(array, LIB, 0, 0, tiled=True)


def tiles_of(array):
    *lead, rows, cols = array.shape
    n = len(lead)
    split = array.reshape(*lead, rows // 8, 8, cols // 128, 128)
    turned = split.transpose(*range(n), n, n + 2, n + 1, n + 3)
    return turned.reshape(*lead, rows // 8, cols // 16, 128)


def outer_columns(halves, lane, spot):
    joined = jnp.where(lane < 64, halves[0], halves[1])
    return pltpu.roll(joined, 4 + 8 * spot, 1)


def columns_of_eight(rows, maps):
    lane = lax.broadcasted_iota(jnp.int32, (maps, 128), 1)
    total = outer_columns(rows(0), lane, 0)
    for j in range(1, 8):
        total = jnp.where(lane // 8 == j, outer_columns(rows(j), lane, j), total)
    return total.T[:64]


def front_kernel(with_compact, *refs):
    in_ref, by_row, refs = refs[0], refs[-1], refs[1 if with_compact else 2 : -1]
    in_ref = in_ref if with_compact else in_ref.at[0]
    maps = in_ref.shape[0]
    for at in range(0, maps, 8):
        for c in range(2):
            tile = jnp.swapaxes(in_ref[at : at + 8, 0, 8 * c : 8 * c + 8, :], 0, 1)
            by_row[:, at : at + 8, 128 * c : 128 * c + 128] = tile

    def rows(j):
        return [by_row[j, :, 128 * c : 128 * c + 128] for c in range(2)]

    if with_compact:
        library, out = refs[0], refs[1]
        share = (out.shape[1] - library.shape[0] // 2) // maps
        height = 8 * share
        for j in range(8):
            row = pl.program_id(0) * 8 + j
            inner = jnp.clip(row - 4, 0, height - 9)
            outer = (row < 4) | (row >= height - 4)
            owner = jnp.where(outer, jnp.where(row < 4, row, row - height + 8), inner // (share - 1))
            slot = jnp.where(outer, 0, 1 + inner % (share - 1))
            at = pl.ds(pl.multiple_of(slot * maps, maps), maps)
            for c, half in enumerate(rows(j)):
                out[owner, at, pl.ds(128 * c, 128)] = half.astype(BF16)

        @pl.when(pl.program_id(0) == 0)
        def _():
            half = library.shape[0] // 2
            for k in range(8):
                for c in range(2):
                    piece = library[half * c : half * c + half]
                    out[k, pl.ds(share * maps, half), pl.ds(128 * c, 128)] = piece

    else:
        step = pl.program_id(1)
        for at, out, start in ((0, refs[0], 0), (pl.num_programs(1) - 1, refs[1], 4)):

            @pl.when(step == at)
            def _():
                for j in range(4):
                    for c, half in enumerate(rows(start + j)):
                        out[0, j, :, pl.ds(128 * c, 128)] = half.astype(BF16)

    refs[-1][...] = columns_of_eight(rows, maps).reshape(refs[-1].shape)


def front_abundance(abundance, library):
    maps, height, width = abundance.shape
    share = height // 8
    length = share * maps + library.shape[0] // 2
    return pl.pallas_call(
        functools.partial(front_kernel, True),
        grid=(height // 8,),
        out_shape=(
            jax.ShapeDtypeStruct((8, length, width), BF16),
            jax.ShapeDtypeStruct((height, 8, maps), F32),
        ),
        in_specs=[pl.BlockSpec((maps, 1, 16, 128), lambda i: (0, i, 0, 0)), WHOLE],
        out_specs=(
            pl.BlockSpec((8, length, width), lambda i: (0, 0, 0)),
            pl.BlockSpec((8, 8, maps), lambda i: (i, 0, 0)),
        ),
        scratch_shapes=[pltpu.VMEM((8, maps, width), F32)],
        compiler_params=pltpu.CompilerParams(vmem_limit_bytes=56 * MIB),
        name="front_abundance",
    )(tiles_of(abundance), library)


def front_duals(duals, after):
    _, maps, height, width = duals.shape
    return pl.pallas_call(
        functools.partial(front_kernel, False),
        grid=(2, height // 8),
        out_shape=(
            jax.ShapeDtypeStruct((2, 4, maps, width), BF16),
            jax.ShapeDtypeStruct((2, 4, maps, width), BF16),
            jax.ShapeDtypeStruct((2, height, 8, maps), F32),
        ),
        in_specs=[
            pl.BlockSpec((1, maps, 1, 16, 128), lambda k, i: (k, 0, i, 0, 0)),
            pl.BlockSpec(memory_space=pl.ANY),
        ],
        out_specs=(
            pl.BlockSpec((1, 4, maps, width), lambda k, i: (k, 0, 0, 0)),
            pl.BlockSpec((1, 4, maps, width), lambda k, i: (k, 0, 0, 0)),
            pl.BlockSpec((1, 8, 8, maps), lambda k, i: (k, i, 0, 0)),
        ),
        scratch_shapes=[pltpu.VMEM((8, maps, width), F32)],
        compiler_params=pltpu.CompilerParams(vmem_limit_bytes=48 * MIB),
        cost_estimate=pl.CostEstimate(flops=0, bytes_accessed=8_000_000, transcendentals=0),
        name="front_duals",
    )(tiles_of(duals), after)


def middle_kernel(blocks, observed, *refs):
    outer, inner = refs[-2:]
    parts, more, maps, width = inner.shape
    share, bands, _ = observed.shape
    start = share * maps
    lane = lax.broadcasted_iota(jnp.int32, (bands, 128), 1)

    def library(k):
        flat = blocks[k, start:]
        return jnp.concatenate([flat[:, :128], flat[:, 128:]])

    wide = jnp.concatenate([library(k) for k in range(parts)], axis=1)
    tall = jnp.concatenate([library(k).astype(F32).T.astype(BF16) for k in range(parts)])
    packed = jnp.zeros((bands, 128), F32)
    for r in range(share):
        pixels = jnp.concatenate([blocks[k, r * maps : r * maps + maps] for k in range(parts)])
        total = jnp.dot(wide, pixels, preferred_element_type=F32) - observed[r].astype(F32)
        rb = total.astype(BF16)
        d = jnp.dot(tall, rb, preferred_element_type=F32).astype(BF16).reshape(parts, maps, width)
        if r == 0:
            outer[:, :maps] = d
        else:
            inner[:, r - 1] = d
        exact = rb.astype(F32)
        moved = outer_columns([exact[:, :128], exact[:, 128:]], lane, r)
        packed = jnp.where(lane // 8 == r, moved, packed)
    columns = packed.T[: 8 * share].astype(BF16)
    d = jnp.dot(columns, wide, preferred_element_type=F32).astype(BF16)
    half = 4 * share
    for k in range(parts):
        for c in range(2):
            piece = d[half * c : half * c + half, k * maps : k * maps + maps]
            outer[k, pl.ds(maps, half), pl.ds(128 * c, 128)] = piece


def middle(blocks, observed, maps, first):
    share, _, width = observed.shape
    return pl.pallas_call(
        middle_kernel,
        out_shape=(
            jax.ShapeDtypeStruct((8, maps + 4 * share, width), BF16),
            jax.ShapeDtypeStruct((8, share - 1, maps, width), BF16),
        ),
        in_specs=[WHOLE] * 2 + [pl.BlockSpec(memory_space=pl.ANY)] * len(first),
        out_specs=(WHOLE, WHOLE),
        compiler_params=pltpu.CompilerParams(vmem_limit_bytes=16 * MIB),
        name="middle",
    )(blocks, observed, *first)


def below_then_above(array, dim, reach=4):
    size = array.shape[dim]
    below = shifted(lax.slice_in_dim(array, 0, reach, axis=dim), "row", -1)
    above = shifted(lax.slice_in_dim(array, size - reach, size, axis=dim), "row", 1)
    return lax.concatenate([below, above], dim)


def columns_kernel(in_ref, out_ref):
    fields, rows, maps, _ = in_ref.shape
    for k in range(fields):
        for i in range(rows // 8):

            def pair(j):
                row = in_ref[k, 8 * i + j].astype(F32)
                return [row[:, :128], row[:, 128:]]

            out_ref[k, pl.ds(8 * i, 8)] = columns_of_eight(pair, maps).reshape(8, 8, maps)


def outer_columns_of(array, name):
    fields, rows, maps, _ = array.shape
    return pl.pallas_call(
        columns_kernel,
        out_shape=jax.ShapeDtypeStruct((fields, rows, 8, maps), F32),
        in_specs=[WHOLE],
        out_specs=WHOLE,
        compiler_params=pltpu.CompilerParams(vmem_limit_bytes=8 * MIB),
        name=name,
    )(array)


def beside(columns):
    return columns, shifted(columns, "col", 1), shifted(columns, "col", -1)


def tv_kernel(
    origin,
    ab_ref,
    q_ref,
    rim_ref,
    douter_ref,
    dinner_ref,
    drim_ref,
    own_ref,
    left_ref,
    right_ref,
    down_ref,
    dleft_ref,
    dright_ref,
    abn_ref,
    qn_ref,
    lefts,
    rights,
    turn,
):
    block = ab_ref.shape[0]
    rows = ab_ref.shape[1]
    tall = rows + 8
    maps = own_ref.shape[-1]
    first_row, first_col, total_rows, total_cols = (origin[i] for i in range(4))

    @pl.when(pl.program_id(0) == 0)
    def _():
        r = lax.broadcasted_iota(jnp.int32, (tall, 8, maps), 0)
        g = first_row + jnp.where(r < rows + 4, r, r - tall)
        b0 = jnp.where((g >= 0) & (g < total_rows - 1), 1.0, 0.0).astype(F32)
        sub = lax.broadcasted_iota(jnp.int32, (tall, 8, maps), 1)

        def keep(out, values, at):
            turn[...] = values.reshape(tall * 8, maps)
            column = turn[pl.ds(at, tall, 8), :]
            out[...] = column

        def strip(nearer, further, dnearer, dfurther, offset, is_left):
            def pick(i):
                return jnp.where(sub < 4, nearer[i], further[i])

            g = first_col + offset + sub
            b1 = jnp.where((g >= 0) & (g < total_cols - 1), 1.0, 0.0).astype(F32)
            s = 0.5 * pick(0) - 0.05 * jnp.where(sub < 4, dnearer[0], dfurther[0])
            u, v = jnp.clip(pick(1), -b0, b0), jnp.clip(pick(2), -b1, b1)
            for p in range(PASSES):
                if is_left:
                    keep(lefts.at[p], v, 3)
                uu = jnp.concatenate([u[tall - 1 :], u[: tall - 1]], axis=0)
                z = s - 0.125 * (u - uu + (v - pltpu.roll(v, 1, 1)))
                if not is_left:
                    keep(rights.at[p], z, 4)
                zd = jnp.concatenate([z[1:], z[:1]], axis=0)
                zr = pltpu.roll(z, 7, 1)
                u = jnp.clip(u + (zd - z), -b0, b0)
                v = jnp.clip(v + (zr - z), -b1, b1)
            if is_left:
                keep(lefts.at[PASSES], v, 3)

        strip(left_ref, own_ref, dleft_ref, down_ref, -4, True)
        strip(own_ref, right_ref, down_ref, dright_ref, 252, False)

    lane = lax.broadcasted_iota(jnp.int32, (tall, 128), 1)
    at_start, at_end = lane == 0, lane == 127
    b1 = jnp.where(first_col + 128 + lane < total_cols - 1, 1.0, 0.0).astype(F32)
    r = lax.broadcasted_iota(jnp.int32, (tall, 128), 0)
    g = first_row + jnp.where(r < rows + 4, r, r - tall)
    b0 = jnp.where((g >= 0) & (g < total_rows - 1), 1.0, 0.0).astype(F32)

    def by_map(c, h, *pieces):
        cols = pl.ds(128 * c, 128)
        found = [ref[pl.ds(at, n), :, cols].astype(F32)[:, 8 * h : 8 * h + 8] for ref, at, n in pieces]
        return jnp.swapaxes(found[0] if len(found) == 1 else jnp.concatenate(found), 0, 1)

    inner = rows - 8
    descents = [[(douter_ref, 0, 4), (dinner_ref, 0, 4)]]
    descents += [[(dinner_ref, at, 8)] for at in range(4, inner - 4, 8)]
    descents += [[(dinner_ref, inner - 4, 4), (douter_ref, 4, 4)], [(drim_ref, 0, 8)]]

    for h in range(block // 8):
        s, u, v, z = {}, {}, {}, {}
        for c in range(2):
            cols = pl.ds(128 * c, 128)
            d = jnp.concatenate([by_map(c, h, *pieces) for pieces in descents], axis=1)
            rim = [by_map(c, h, (rim_ref.at[i], 0, 8)) for i in range(3)]
            for k in range(8):
                m = 8 * h + k
                main = ab_ref[m, :, cols], q_ref[0, m, :, cols], q_ref[1, m, :, cols]
                full = [jnp.concatenate([main[i], rim[i][k]], axis=0) for i in range(3)]
                s[k, c] = 0.5 * full[0] - 0.05 * d[k]
                u[k, c] = jnp.clip(full[1], -b0, b0)
                v[k, c] = jnp.clip(full[2], -b1, b1) if c else full[2]
        gms = [pl.program_id(0) * block + 8 * h + k for k in range(8)]

        def field(p, k):
            edge = pltpu.roll(lefts[p], lax.rem(128 - gms[k], 128), 1)
            t = [pltpu.roll(v[k, c], 1, 1) for c in range(2)]
            before = jnp.where(at_start, edge, t[0]), jnp.where(at_start, t[0], t[1])
            for c in range(2):
                vertical = u[k, c] - pltpu.roll(u[k, c], 1, 0)
                z[k, c] = s[k, c] - 0.125 * (vertical + (v[k, c] - before[c]))

        for p in range(PASSES):
            for k in range(8):
                field(p, k)
            for k in range(8):
                edge = pltpu.roll(rights[p], 127 - gms[k], 1)
                t = [pltpu.roll(z[k, c], 127, 1) for c in range(2)]
                after = jnp.where(at_end, t[1], t[0]), jnp.where(at_end, edge, t[1])
                for c in range(2):
                    below = pltpu.roll(z[k, c], tall - 1, 0)
                    bound = b1 if c else 1.0
                    u[k, c] = jnp.clip(u[k, c] + (below - z[k, c]), -b0, b0)
                    v[k, c] = jnp.clip(v[k, c] + (after[c] - z[k, c]), -bound, bound)
        for k in range(8):
            field(PASSES, k)
            m = 8 * h + k
            for c in range(2):
                cols = pl.ds(128 * c, 128)
                abn_ref[m, :, cols] = jnp.maximum(2.0 * z[k, c][:rows] - 0.02, 0.0)
                qn_ref[0, m, :, cols] = u[k, c][:rows]
                qn_ref[1, m, :, cols] = v[k, c][:rows]


def tv(origin, abundance, duals, rim, douter, dinner, drim, strips, dstrips):
    maps, rows, cols = abundance.shape
    block = 16
    tall = rows + 8
    tile = pl.BlockSpec((block, rows, cols), lambda i: (i, 0, 0))
    pair = pl.BlockSpec((2, block, rows, cols), lambda i: (0, i, 0, 0))

    def by_row(count):
        return pl.BlockSpec((count, block, cols), lambda i: (0, i, 0))

    return pl.pallas_call(
        tv_kernel,
        grid=(maps // block,),
        out_shape=(
            jax.ShapeDtypeStruct(abundance.shape, F32),
            jax.ShapeDtypeStruct(duals.shape, F32),
        ),
        in_specs=[
            SCALARS,
            tile,
            pair,
            pl.BlockSpec((3, 8, block, cols), lambda i: (0, 0, i, 0)),
            by_row(8),
            by_row(rows - 8),
            by_row(8),
        ]
        + [WHOLE] * 6,
        out_specs=(tile, pair),
        scratch_shapes=[
            pltpu.VMEM((PASSES + 1, tall, maps), F32),
            pltpu.VMEM((PASSES, tall, maps), F32),
            pltpu.VMEM((tall * 8, maps), F32),
        ],
        compiler_params=pltpu.CompilerParams(vmem_limit_bytes=52 * MIB),
        name="tv",
    )(origin, abundance, duals, rim, douter, dinner, drim, *strips, *dstrips)


def on_device(abundance, duals, reflectance, library):
    maps, height, width = abundance.shape
    share = height // 8
    me = lax.axis_index(LIB)
    compact, columns = front_abundance(abundance, library)
    blocks = to_all(compact)
    outer_row = jnp.where(me < 4, me, me + height - 8)
    observed = [
        lax.dynamic_slice_in_dim(reflectance, outer_row, 1, 1),
        lax.dynamic_slice_in_dim(reflectance, 4 + me * (share - 1), share - 1, 1),
    ]
    observed = jnp.concatenate(observed, axis=1).transpose(1, 0, 2)

    first, last, dual_columns = front_duals(duals, compact)
    first = jnp.concatenate([compact[None, :4, :maps], first])
    last = jnp.concatenate([compact[None, 4:, :maps], last])
    rim = jnp.concatenate([shifted(first, "row", -1), shifted(last, "row", 1)], axis=1)
    columns = jnp.concatenate([columns[None], dual_columns], axis=0)
    strips = beside(jnp.concatenate([columns, outer_columns_of(rim, "rim_columns")], axis=1))

    outer, inner = middle(blocks, observed, maps, [rim])
    outer = to_all(outer)
    inner, outer, strips = lax.optimization_barrier((inner, outer, strips))
    dinner = to_all(inner).reshape(height - 8, maps, width)
    douter = outer[:, :maps]
    sides = [half.reshape(8, share // 2, 8, maps) for half in jnp.split(outer[:, maps:], 2, axis=2)]
    sides = jnp.concatenate(sides, axis=1).astype(F32)
    middle_rows = sides[:, 1:].reshape(height - 8, 8, maps)
    drim = below_then_above(douter, 0)
    above = outer_columns_of(drim[None], "descent_rim_columns")[0]
    dstrips = beside(jnp.concatenate([sides[:4, 0], middle_rows, sides[4:, 0], above])[None])
    origin = jnp.stack(
        [
            lax.axis_index("row") * height,
            lax.axis_index("col") * width,
            height * lax.axis_size("row"),
            width * lax.axis_size("col"),
        ]
    )
    return tv(origin, abundance, duals, rim, douter, dinner, drim, strips, dstrips)


def solution(mesh):
    torus = Mesh(
        mesh.devices.reshape(4, 2, mesh.shape["row"], mesh.shape["col"]),
        ("lib_0", "lib_1", "row", "col"),
    )
    placed = (P(LIB, "row", "col"), P(None, LIB, "row", "col"), P(None, "row", "col"), P(None, LIB))
    return jax.shard_map(
        on_device,
        mesh=torus,
        in_specs=placed,
        out_specs=(P(LIB, "row", "col"), P(None, LIB, "row", "col")),
        check_vma=False,
    )
```

```python
import functools

import jax
import jax.numpy as jnp
from jax import lax
from jax.experimental import pallas as pl
from jax.experimental.pallas import tpu as pltpu
from jax.sharding import Mesh
from jax.sharding import PartitionSpec as P

PASSES = 3
LIB = ("lib_0", "lib_1")
BF16 = jnp.bfloat16
F32 = jnp.float32
MIB = 1024 * 1024
WHOLE = pl.BlockSpec(memory_space=pltpu.VMEM)
SCALARS = pl.BlockSpec(memory_space=pltpu.SMEM)


def shifted(array, axis, by):
    length = lax.axis_size(axis)
    pairs = [(i, i + by) for i in range(length) if 0 <= i + by < length]
    return lax.ppermute(array, axis, pairs)


def to_all(array):
    return lax.all_to_all(array, LIB, 0, 0, tiled=True)


def tiles_of(array):
    *lead, rows, cols = array.shape
    n = len(lead)
    split = array.reshape(*lead, rows // 8, 8, cols // 128, 128)
    turned = split.transpose(*range(n), n, n + 2, n + 1, n + 3)
    return turned.reshape(*lead, rows // 8, cols // 16, 128)


def outer_columns(halves, lane, spot):
    joined = jnp.where(lane < 64, halves[0], halves[1])
    return pltpu.roll(joined, 4 + 8 * spot, 1)


def columns_of_eight(rows, maps):
    lane = lax.broadcasted_iota(jnp.int32, (maps, 128), 1)
    total = outer_columns(rows(0), lane, 0)
    for j in range(1, 8):
        total = jnp.where(lane // 8 == j, outer_columns(rows(j), lane, j), total)
    return total.T[:64]


def front_kernel(with_compact, *refs):
    in_ref, by_row, refs = refs[0], refs[-1], refs[1 if with_compact else 2 : -1]
    in_ref = in_ref if with_compact else in_ref.at[0]
    maps = in_ref.shape[0]
    for at in range(0, maps, 8):
        for c in range(2):
            tile = jnp.swapaxes(in_ref[at : at + 8, 0, 8 * c : 8 * c + 8, :], 0, 1)
            by_row[:, at : at + 8, 128 * c : 128 * c + 128] = tile

    def rows(j):
        return [by_row[j, :, 128 * c : 128 * c + 128] for c in range(2)]

    if with_compact:
        library, out = refs[0], refs[1]
        share = (out.shape[1] - library.shape[0] // 2) // maps
        height = 8 * share
        for j in range(8):
            row = pl.program_id(0) * 8 + j
            inner = jnp.clip(row - 4, 0, height - 9)
            outer = (row < 4) | (row >= height - 4)
            owner = jnp.where(outer, jnp.where(row < 4, row, row - height + 8), inner // (share - 1))
            slot = jnp.where(outer, 0, 1 + inner % (share - 1))
            at = pl.ds(pl.multiple_of(slot * maps, maps), maps)
            for c, half in enumerate(rows(j)):
                out[owner, at, pl.ds(128 * c, 128)] = half.astype(BF16)

        @pl.when(pl.program_id(0) == 0)
        def _():
            half = library.shape[0] // 2
            for k in range(8):
                for c in range(2):
                    piece = library[half * c : half * c + half]
                    out[k, pl.ds(share * maps, half), pl.ds(128 * c, 128)] = piece

    else:
        step = pl.program_id(1)
        for at, out, start in ((0, refs[0], 0), (pl.num_programs(1) - 1, refs[1], 4)):

            @pl.when(step == at)
            def _():
                for j in range(4):
                    for c, half in enumerate(rows(start + j)):
                        out[0, j, :, pl.ds(128 * c, 128)] = half.astype(BF16)

    refs[-1][...] = columns_of_eight(rows, maps).reshape(refs[-1].shape)


def front_abundance(abundance, library):
    maps, height, width = abundance.shape
    share = height // 8
    length = share * maps + library.shape[0] // 2
    return pl.pallas_call(
        functools.partial(front_kernel, True),
        grid=(height // 8,),
        out_shape=(
            jax.ShapeDtypeStruct((8, length, width), BF16),
            jax.ShapeDtypeStruct((height, 8, maps), F32),
        ),
        in_specs=[pl.BlockSpec((maps, 1, 16, 128), lambda i: (0, i, 0, 0)), WHOLE],
        out_specs=(
            pl.BlockSpec((8, length, width), lambda i: (0, 0, 0)),
            pl.BlockSpec((8, 8, maps), lambda i: (i, 0, 0)),
        ),
        scratch_shapes=[pltpu.VMEM((8, maps, width), F32)],
        compiler_params=pltpu.CompilerParams(vmem_limit_bytes=56 * MIB),
        name="front_abundance",
    )(tiles_of(abundance), library)


def front_duals(duals, after):
    _, maps, height, width = duals.shape
    return pl.pallas_call(
        functools.partial(front_kernel, False),
        grid=(2, height // 8),
        out_shape=(
            jax.ShapeDtypeStruct((2, 4, maps, width), BF16),
            jax.ShapeDtypeStruct((2, 4, maps, width), BF16),
            jax.ShapeDtypeStruct((2, height, 8, maps), F32),
        ),
        in_specs=[
            pl.BlockSpec((1, maps, 1, 16, 128), lambda k, i: (k, 0, i, 0, 0)),
            pl.BlockSpec(memory_space=pl.ANY),
        ],
        out_specs=(
            pl.BlockSpec((1, 4, maps, width), lambda k, i: (k, 0, 0, 0)),
            pl.BlockSpec((1, 4, maps, width), lambda k, i: (k, 0, 0, 0)),
            pl.BlockSpec((1, 8, 8, maps), lambda k, i: (k, i, 0, 0)),
        ),
        scratch_shapes=[pltpu.VMEM((8, maps, width), F32)],
        compiler_params=pltpu.CompilerParams(vmem_limit_bytes=48 * MIB),
        cost_estimate=pl.CostEstimate(flops=0, bytes_accessed=8_000_000, transcendentals=0),
        name="front_duals",
    )(tiles_of(duals), after)


def middle_kernel(blocks, observed, *refs):
    outer, inner = refs[-2:]
    parts, more, maps, width = inner.shape
    share, bands, _ = observed.shape
    start = share * maps
    lane = lax.broadcasted_iota(jnp.int32, (bands, 128), 1)

    def library(k):
        flat = blocks[k, start:]
        return jnp.concatenate([flat[:, :128], flat[:, 128:]])

    wide = jnp.concatenate([library(k) for k in range(parts)], axis=1)
    tall = jnp.concatenate([library(k).astype(F32).T.astype(BF16) for k in range(parts)])
    packed = jnp.zeros((bands, 128), F32)
    for r in range(share):
        pixels = jnp.concatenate([blocks[k, r * maps : r * maps + maps] for k in range(parts)])
        total = jnp.dot(wide, pixels, preferred_element_type=F32) - observed[r].astype(F32)
        rb = total.astype(BF16)
        d = jnp.dot(tall, rb, preferred_element_type=F32).astype(BF16).reshape(parts, maps, width)
        if r == 0:
            outer[:, :maps] = d
        else:
            inner[:, r - 1] = d
        exact = rb.astype(F32)
        moved = outer_columns([exact[:, :128], exact[:, 128:]], lane, r)
        packed = jnp.where(lane // 8 == r, moved, packed)
    columns = packed.T[: 8 * share].astype(BF16)
    d = jnp.dot(columns, wide, preferred_element_type=F32).astype(BF16)
    half = 4 * share
    for k in range(parts):
        for c in range(2):
            piece = d[half * c : half * c + half, k * maps : k * maps + maps]
            outer[k, pl.ds(maps, half), pl.ds(128 * c, 128)] = piece


def middle(blocks, observed, maps, first):
    share, _, width = observed.shape
    return pl.pallas_call(
        middle_kernel,
        out_shape=(
            jax.ShapeDtypeStruct((8, maps + 4 * share, width), BF16),
            jax.ShapeDtypeStruct((8, share - 1, maps, width), BF16),
        ),
        in_specs=[WHOLE] * 2 + [pl.BlockSpec(memory_space=pl.ANY)] * len(first),
        out_specs=(WHOLE, WHOLE),
        compiler_params=pltpu.CompilerParams(vmem_limit_bytes=56 * MIB),
        name="middle",
    )(blocks, observed, *first)


def below_then_above(array, dim, reach=4):
    size = array.shape[dim]
    below = shifted(lax.slice_in_dim(array, 0, reach, axis=dim), "row", -1)
    above = shifted(lax.slice_in_dim(array, size - reach, size, axis=dim), "row", 1)
    return lax.concatenate([below, above], dim)


def columns_kernel(in_ref, out_ref):
    fields, rows, maps, _ = in_ref.shape
    for k in range(fields):
        for i in range(rows // 8):

            def pair(j):
                row = in_ref[k, 8 * i + j].astype(F32)
                return [row[:, :128], row[:, 128:]]

            out_ref[k, pl.ds(8 * i, 8)] = columns_of_eight(pair, maps).reshape(8, 8, maps)


def outer_columns_of(array, name):
    fields, rows, maps, _ = array.shape
    return pl.pallas_call(
        columns_kernel,
        out_shape=jax.ShapeDtypeStruct((fields, rows, 8, maps), F32),
        in_specs=[WHOLE],
        out_specs=WHOLE,
        compiler_params=pltpu.CompilerParams(vmem_limit_bytes=8 * MIB),
        name=name,
    )(array)


def beside(columns):
    return columns, shifted(columns, "col", 1), shifted(columns, "col", -1)


def tv_kernel(
    origin,
    ab_ref,
    q_ref,
    rim_ref,
    douter_ref,
    dinner_ref,
    drim_ref,
    own_ref,
    left_ref,
    right_ref,
    down_ref,
    dleft_ref,
    dright_ref,
    abn_ref,
    qn_ref,
    lefts,
    rights,
    turn,
):
    block = ab_ref.shape[0]
    rows = ab_ref.shape[1]
    tall = rows + 8
    maps = own_ref.shape[-1]
    first_row, first_col, total_rows, total_cols = (origin[i] for i in range(4))

    @pl.when(pl.program_id(0) == 0)
    def _():
        r = lax.broadcasted_iota(jnp.int32, (tall, 8, maps), 0)
        g = first_row + jnp.where(r < rows + 4, r, r - tall)
        b0 = jnp.where((g >= 0) & (g < total_rows - 1), 1.0, 0.0).astype(F32)
        sub = lax.broadcasted_iota(jnp.int32, (tall, 8, maps), 1)

        def keep(out, values, at):
            turn[...] = values.reshape(tall * 8, maps)
            column = turn[pl.ds(at, tall, 8), :]
            out[...] = column

        def strip(nearer, further, dnearer, dfurther, offset, is_left):
            def pick(i):
                return jnp.where(sub < 4, nearer[i], further[i])

            g = first_col + offset + sub
            b1 = jnp.where((g >= 0) & (g < total_cols - 1), 1.0, 0.0).astype(F32)
            s = 0.5 * pick(0) - 0.05 * jnp.where(sub < 4, dnearer[0], dfurther[0])
            u, v = jnp.clip(pick(1), -b0, b0), jnp.clip(pick(2), -b1, b1)
            for p in range(PASSES):
                if is_left:
                    keep(lefts.at[p], v, 3)
                uu = jnp.concatenate([u[tall - 1 :], u[: tall - 1]], axis=0)
                z = s - 0.125 * (u - uu + (v - pltpu.roll(v, 1, 1)))
                if not is_left:
                    keep(rights.at[p], z, 4)
                zd = jnp.concatenate([z[1:], z[:1]], axis=0)
                zr = pltpu.roll(z, 7, 1)
                u = jnp.clip(u + (zd - z), -b0, b0)
                v = jnp.clip(v + (zr - z), -b1, b1)
            if is_left:
                keep(lefts.at[PASSES], v, 3)

        strip(left_ref, own_ref, dleft_ref, down_ref, -4, True)
        strip(own_ref, right_ref, down_ref, dright_ref, 252, False)

    lane = lax.broadcasted_iota(jnp.int32, (tall, 128), 1)
    at_start, at_end = lane == 0, lane == 127
    b1 = jnp.where(first_col + 128 + lane < total_cols - 1, 1.0, 0.0).astype(F32)
    r = lax.broadcasted_iota(jnp.int32, (tall, 128), 0)
    g = first_row + jnp.where(r < rows + 4, r, r - tall)
    b0 = jnp.where((g >= 0) & (g < total_rows - 1), 1.0, 0.0).astype(F32)

    def by_map(c, h, *pieces):
        cols = pl.ds(128 * c, 128)
        found = [ref[pl.ds(at, n), :, cols].astype(F32)[:, 8 * h : 8 * h + 8] for ref, at, n in pieces]
        return jnp.swapaxes(found[0] if len(found) == 1 else jnp.concatenate(found), 0, 1)

    inner = rows - 8
    descents = [[(douter_ref, 0, 4), (dinner_ref, 0, 4)]]
    descents += [[(dinner_ref, at, 8)] for at in range(4, inner - 4, 8)]
    descents += [[(dinner_ref, inner - 4, 4), (douter_ref, 4, 4)], [(drim_ref, 0, 8)]]

    for h in range(block // 8):
        s, u, v, z = {}, {}, {}, {}
        for c in range(2):
            cols = pl.ds(128 * c, 128)
            d = jnp.concatenate([by_map(c, h, *pieces) for pieces in descents], axis=1)
            rim = [by_map(c, h, (rim_ref.at[i], 0, 8)) for i in range(3)]
            for k in range(8):
                m = 8 * h + k
                main = ab_ref[m, :, cols], q_ref[0, m, :, cols], q_ref[1, m, :, cols]
                full = [jnp.concatenate([main[i], rim[i][k]], axis=0) for i in range(3)]
                s[k, c] = 0.5 * full[0] - 0.05 * d[k]
                u[k, c] = jnp.clip(full[1], -b0, b0)
                v[k, c] = jnp.clip(full[2], -b1, b1) if c else full[2]
        gms = [pl.program_id(0) * block + 8 * h + k for k in range(8)]

        def field(p, k):
            edge = pltpu.roll(lefts[p], lax.rem(128 - gms[k], 128), 1)
            t = [pltpu.roll(v[k, c], 1, 1) for c in range(2)]
            before = jnp.where(at_start, edge, t[0]), jnp.where(at_start, t[0], t[1])
            for c in range(2):
                vertical = u[k, c] - pltpu.roll(u[k, c], 1, 0)
                z[k, c] = s[k, c] - 0.125 * (vertical + (v[k, c] - before[c]))

        for p in range(PASSES):
            for k in range(8):
                field(p, k)
            for k in range(8):
                edge = pltpu.roll(rights[p], 127 - gms[k], 1)
                t = [pltpu.roll(z[k, c], 127, 1) for c in range(2)]
                after = jnp.where(at_end, t[1], t[0]), jnp.where(at_end, edge, t[1])
                for c in range(2):
                    below = pltpu.roll(z[k, c], tall - 1, 0)
                    bound = b1 if c else 1.0
                    u[k, c] = jnp.clip(u[k, c] + (below - z[k, c]), -b0, b0)
                    v[k, c] = jnp.clip(v[k, c] + (after[c] - z[k, c]), -bound, bound)
        for k in range(8):
            field(PASSES, k)
            m = 8 * h + k
            for c in range(2):
                cols = pl.ds(128 * c, 128)
                abn_ref[m, :, cols] = jnp.maximum(2.0 * z[k, c][:rows] - 0.02, 0.0)
                qn_ref[0, m, :, cols] = u[k, c][:rows]
                qn_ref[1, m, :, cols] = v[k, c][:rows]


def tv(origin, abundance, duals, rim, douter, dinner, drim, strips, dstrips):
    maps, rows, cols = abundance.shape
    block = 16
    tall = rows + 8
    tile = pl.BlockSpec((block, rows, cols), lambda i: (i, 0, 0))
    pair = pl.BlockSpec((2, block, rows, cols), lambda i: (0, i, 0, 0))

    def by_row(count):
        return pl.BlockSpec((count, block, cols), lambda i: (0, i, 0))

    return pl.pallas_call(
        tv_kernel,
        grid=(maps // block,),
        out_shape=(
            jax.ShapeDtypeStruct(abundance.shape, F32),
            jax.ShapeDtypeStruct(duals.shape, F32),
        ),
        in_specs=[
            SCALARS,
            tile,
            pair,
            pl.BlockSpec((3, 8, block, cols), lambda i: (0, 0, i, 0)),
            by_row(8),
            by_row(rows - 8),
            by_row(8),
        ]
        + [WHOLE] * 6,
        out_specs=(tile, pair),
        scratch_shapes=[
            pltpu.VMEM((PASSES + 1, tall, maps), F32),
            pltpu.VMEM((PASSES, tall, maps), F32),
            pltpu.VMEM((tall * 8, maps), F32),
        ],
        compiler_params=pltpu.CompilerParams(vmem_limit_bytes=52 * MIB),
        name="tv",
    )(origin, abundance, duals, rim, douter, dinner, drim, *strips, *dstrips)


def on_device(abundance, duals, reflectance, library):
    maps, height, width = abundance.shape
    share = height // 8
    me = lax.axis_index(LIB)
    compact, columns = front_abundance(abundance, library)
    blocks = to_all(compact)
    outer_row = jnp.where(me < 4, me, me + height - 8)
    observed = [
        lax.dynamic_slice_in_dim(reflectance, outer_row, 1, 1),
        lax.dynamic_slice_in_dim(reflectance, 4 + me * (share - 1), share - 1, 1),
    ]
    observed = jnp.concatenate(observed, axis=1).transpose(1, 0, 2)

    first, last, dual_columns = front_duals(duals, compact)
    first = jnp.concatenate([compact[None, :4, :maps], first])
    last = jnp.concatenate([compact[None, 4:, :maps], last])
    rim = jnp.concatenate([shifted(first, "row", -1), shifted(last, "row", 1)], axis=1)
    columns = jnp.concatenate([columns[None], dual_columns], axis=0)
    strips = beside(jnp.concatenate([columns, outer_columns_of(rim, "rim_columns")], axis=1))

    outer, inner = middle(blocks, observed, maps, [rim])
    outer = to_all(outer)
    inner, outer, strips = lax.optimization_barrier((inner, outer, strips))
    dinner = to_all(inner).reshape(height - 8, maps, width)
    douter = outer[:, :maps]
    sides = [half.reshape(8, share // 2, 8, maps) for half in jnp.split(outer[:, maps:], 2, axis=2)]
    sides = jnp.concatenate(sides, axis=1).astype(F32)
    middle_rows = sides[:, 1:].reshape(height - 8, 8, maps)
    drim = below_then_above(douter, 0)
    above = outer_columns_of(drim[None], "descent_rim_columns")[0]
    dstrips = beside(jnp.concatenate([sides[:4, 0], middle_rows, sides[4:, 0], above])[None])
    origin = jnp.stack(
        [
            lax.axis_index("row") * height,
            lax.axis_index("col") * width,
            height * lax.axis_size("row"),
            width * lax.axis_size("col"),
        ]
    )
    return tv(origin, abundance, duals, rim, douter, dinner, drim, strips, dstrips)


def solution(mesh):
    torus = Mesh(
        mesh.devices.reshape(4, 2, mesh.shape["row"], mesh.shape["col"]),
        ("lib_0", "lib_1", "row", "col"),
    )
    placed = (P(LIB, "row", "col"), P(None, LIB, "row", "col"), P(None, "row", "col"), P(None, LIB))
    return jax.shard_map(
        on_device,
        mesh=torus,
        in_specs=placed,
        out_specs=(P(LIB, "row", "col"), P(None, LIB, "row", "col")),
        check_vma=False,
    )
```
